256 devices in a mesh: dp: 8 (over y, core), mp: 32 (over x, z).
Axes of the slice: x: 4, y: 4, z: 8, core: 2. Of those that a mesh axis runs over, the one named last changes fastest.
Arguments:
- tokens: bfloat16 [4096, 8192], P('dp', 'mp'), may hold values from -6 to 6
- base_weight: bfloat16 [8192, 8192], P(None, 'mp'), may hold values from -0.0625 to 0.0625
- adapter_pairs: bfloat16 [64, 8192, 128], P('mp'), as said below
- owner_map: int32 [64], replicated, may hold values from 0 to 63, each once
- seg_adapter: int32 [8, 4], replicated, may hold values from 0 to 63
- seg_lengths: int32 [8, 4], P('dp'), may hold values from 1 to 256, 512 in all within a row
- cotangent: bfloat16 [4096, 8192], P('dp', 'mp'), may hold values from -6 to 6
Outputs:
- output: bfloat16 [4096, 8192], P('dp', 'mp')
- input_grad: bfloat16 [4096, 8192], P('dp', 'mp')
- adapter_grad: float32 [64, 8192, 128], P('dp', 'mp')
The draws below stay inside these ranges and needn't reach their ends.
Inputs may be any that keep to these rules, and one draw needn't show every extreme that they name: `owner_map`: slot p lives on mp index p // 2; every slot belongs to exactly one adapter. `adapter_pairs`: the first 64 columns of the last dimension hold the down projections, the last 64 the transposed up projections.
All inputs are finite; a program needn't handle non-finite values.
Results may differ from the reference program's by a relative error of at most 0.009.
Values may be sent and summed in bfloat16 or wider, within the bound.
A program may use at most 128 MiB of HBM per device.

```python
import math
import jax
import jax.numpy as jnp
import numpy as np
from jax import lax

D = 8192
R = 64
SEGS = 4
TOK_DEV = 512
ADAPTERS = 64
TOKENS = 4096
N_DP = 8
N_MP = 32


def draw_adapter_pairs(key, part):
    key = jax.random.fold_in(key, 11)
    values = jax.random.normal(key, (ADAPTERS, D, 2 * R), jnp.float32)
    scales = jnp.concatenate([jnp.full((R,), D ** (-0.5), jnp.float32), jnp.full((R,), R ** (-0.5), jnp.float32)])
    return (values * scales[None, None, :]).astype(jnp.bfloat16)


def touch_ends(entries, own_key, smallest, high):
    dims = entries.shape
    place = [jax.random.randint(jax.random.fold_in(own_key, axis), (), 0, dims[axis]) for axis in range(len(dims))]
    entries = entries.at[tuple(place)].set(smallest)
    longest = dims.index(max(dims))
    place[longest] = (place[longest] + 1) % dims[longest]
    return entries.at[tuple(place)].set(high)


def level_of(key, shape, shards, smallest, high):
    loudness, own = 1.0, jax.random.fold_in(key, 6)
    for dim, blocks in shards:
        draws = jnp.exp(jax.random.uniform(jax.random.fold_in(own, dim), (blocks,), jnp.float32, smallest / len(shards), high / len(shards)))
        loudness = loudness * jnp.repeat(draws, shape[dim] // blocks).reshape([-1 if axis == dim else 1 for axis in range(len(shape))])
    return loudness


def profile(number_of, total, bound, skew):
    weights = [(1 << 20) // math.isqrt(standing ** skew) + 1 for standing in range(2, number_of + 1)]
    rest, counts = total - bound - (number_of - 1), [1] * (number_of - 1)
    while rest > 0:
        candidates = [i for i in range(number_of - 1) if counts[i] < bound]
        whole, budget = sum([weights[i] for i in candidates]), rest
        for i in candidates:
            extra = min(bound - counts[i], max(1, budget * weights[i] // whole), rest)
            counts[i] = counts[i] + extra
            rest = rest - extra
    return np.array([bound] + counts)


def ragged(stream_key, amount, total, limit, skew):
    if amount == 2:
        one = jax.random.randint(stream_key, (), max(1, total - limit), min(limit, total - 1) + 1)
        return jnp.stack([one, total - one])
    sizes = jnp.asarray(profile(amount, total, limit, skew), jnp.int32)
    twos = (amount - 1) // 2
    donor, sink = sizes[1:1 + 2 * twos:2], sizes[2:2 + 2 * twos:2]
    room = jnp.minimum(donor - 1, limit - sink)
    shifted = jax.random.randint(jax.random.fold_in(stream_key, 1), (twos,), 0, 1 << 20) % (room + 1)
    sizes = sizes.at[1:1 + 2 * twos:2].set(donor - shifted).at[2:2 + 2 * twos:2].set(sink + shifted)
    return sizes[jax.random.permutation(jax.random.fold_in(stream_key, 2), amount)]


def gaussian(own_key, extent, spread, limit, cuts=(), kind=jnp.bfloat16):
    values = jax.random.normal(own_key, extent, jnp.float32) * spread
    if len(cuts) > 0:
        values = level_of(own_key, extent, cuts, -0.22, 0.18) * values
    return jnp.clip(values, min=-limit, max=limit).astype(kind)


def setup_inputs(seed: int = 0) -> dict:
    arg_keys = jax.random.split(jax.random.key(seed), 8)
    tokens = gaussian(arg_keys[0], (TOKENS, D), 1.0, 6.0, ((0, 8), (1, 32)))
    base_weight = gaussian(arg_keys[1], (D, D), D ** -0.5, 0.0625, ((1, 32),))
    adapter_pairs = draw_adapter_pairs(jax.random.fold_in(arg_keys[7], 71), 0)
    owner_map = jax.random.permutation(arg_keys[3], ADAPTERS).astype(jnp.int32)
    seg_adapter = touch_ends(jax.random.randint(arg_keys[4], (N_DP, SEGS), 0, ADAPTERS), jax.random.fold_in(arg_keys[4], 1), 0, ADAPTERS - 1).astype(jnp.int32)
    seg_lengths = jax.vmap(lambda own: ragged(own, SEGS, TOK_DEV, TOK_DEV // 2, 2))(jax.random.split(arg_keys[5], N_DP)).reshape((N_DP, SEGS)).astype(jnp.int32)
    cotangent = gaussian(arg_keys[6], (TOKENS, D), 1.0, 6.0, ((0, 8), (1, 32)))
    return {"tokens": tokens, "base_weight": base_weight, "adapter_pairs": adapter_pairs, "owner_map": owner_map, "seg_adapter": seg_adapter, "seg_lengths": seg_lengths, "cotangent": cotangent}


def reference(tokens, base_weight, adapter_pairs, owner_map, seg_adapter, seg_lengths, cotangent):
    block = D // N_MP

    def micro(grad, index):
        start = (index * TOK_DEV).astype(jnp.int32)
        rows = lax.dynamic_slice_in_dim(tokens, start, TOK_DEV, 0)
        grads_in = lax.dynamic_slice_in_dim(cotangent, start, TOK_DEV, 0)
        lengths = seg_lengths[index]
        ends = jnp.cumsum(lengths)
        position = jnp.arange(TOK_DEV, dtype=jnp.int32)
        seg_row = jnp.sum((position[:, None] >= ends[None, :]).astype(jnp.int32), axis=1)
        mask = (seg_row[:, None] == jnp.arange(SEGS, dtype=jnp.int32)[None, :]).astype(jnp.float32)
        slots = owner_map[seg_adapter[index]].astype(jnp.int32)
        pairs = adapter_pairs[slots].astype(jnp.float32)
        down = pairs[:, :, :R]
        upper = pairs[:, :, R:]
        rows_f = rows.astype(jnp.float32)
        grads_f = grads_in.astype(jnp.float32)
        low = jnp.sum(jnp.einsum('tf,sfr->tsr', rows_f, down) * mask[:, :, None], axis=1).astype(jnp.bfloat16)
        back = jnp.sum(jnp.einsum('tf,sfr->tsr', grads_f, upper) * mask[:, :, None], axis=1).astype(jnp.bfloat16)
        low_m = low.astype(jnp.float32)[:, None, :] * mask[:, :, None]
        back_m = back.astype(jnp.float32)[:, None, :] * mask[:, :, None]
        base = jnp.dot(rows, base_weight, preferred_element_type=jnp.float32)
        output = (base + jnp.einsum('tsr,sdr->td', low_m, upper)).astype(jnp.bfloat16)

        def part(total, column):
            offset = (column * block).astype(jnp.int32)
            cols = lax.dynamic_slice_in_dim(grads_in, offset, block, 1)
            wcols = lax.dynamic_slice_in_dim(base_weight, offset, block, 1)
            term = lax.dot_general(cols, wcols, (((1,), (1,)), ((), ())), preferred_element_type=jnp.float32)
            return total + term, None

        total, _ = lax.scan(part, jnp.zeros((TOK_DEV, D), jnp.float32), jnp.arange(N_MP, dtype=jnp.int32))
        input_grad = (total + jnp.einsum('tsr,sfr->tf', back_m, down)).astype(jnp.bfloat16)
        grad_down = jnp.einsum('tf,tsr->sfr', rows_f, back_m)
        grad_up = jnp.einsum('tf,tsr->sfr', grads_f, low_m)
        grad = grad.at[slots].add(jnp.concatenate([grad_down, grad_up], axis=-1))
        return grad, (output, input_grad)

    grad, (outputs, input_grads) = lax.scan(micro, jnp.zeros((ADAPTERS, D, 2 * R), jnp.float32), jnp.arange(N_DP, dtype=jnp.int32))
    return outputs.reshape(N_DP * TOK_DEV, D), input_grads.reshape(N_DP * TOK_DEV, D), grad
```

```python
import functools

import jax
import jax.numpy as jnp
from jax import lax
from jax.experimental import pallas as pl
from jax.experimental.pallas import tpu as pltpu
from jax.sharding import PartitionSpec as P

NZ = 8
CORES = 2
F32 = jnp.float32
BF16 = jnp.bfloat16
NT = (((1,), (1,)), ((), ()))
TN = (((0,), (0,)), ((), ()))


def dot(a, b, dims=(((1,), (0,)), ((), ()))):
    return lax.dot_general(a, b, dims, preferred_element_type=F32)


def hops(n, way, half):
    return n // 2 if way == half else n // 2 - 1


def kernel(
    nx, nz, ny,
    tok, cot, w, pairs, owner, seg, lens,
    out, ig, grad,
    T, C, Wb, S1, S2, sel, R, Lp, X1, Lz, Z1, Lf, Lm, acc, Pz, zs, zr, xs, xr, G,
    t_s, t_r, c_s, c_r, wx_s, wx_r, wy_s, wy_r, wc_s, wc_r,
    a1_s, a1_r, a2_s, a2_r, a3_s, a3_r,
    l1_s, l1_r, l2_s, l2_r, l3_s, l3_r, l4_s, l4_r,
    rz_s, rz_r, rx_s, rx_r, gy_s, gy_r, gc_s, gc_r, loc,
):
    nd = ny * CORES
    d = lax.axis_index("dp")
    j = lax.axis_index("mp")
    y, c = d // CORES, d % CORES
    x, z = j // nz, j % nz
    half_rows, feat = tok.shape[1], tok.shape[2]
    rows = 2 * half_rows
    lanes = 2 * (pairs.shape[-1] // 2)
    rank = lanes // 2
    segs = R.shape[0]
    sibling = (CORES * y + 1 - c, j)

    def at_x(r):
        return (d, lax.rem(r + nx, nx) * nz + z)

    def at_z(r):
        return (d, x * nz + lax.rem(r + nz, nz))

    def at_y(r):
        return (lax.rem(r + ny, ny) * CORES + c, j)

    def at_dp(r):
        return (lax.rem(r + nd, nd), j)

    pending = []

    def remote(src, dst, ssem, rsem, device):
        return pltpu.make_async_remote_copy(
            src_ref=src, dst_ref=dst, send_sem=ssem, recv_sem=rsem,
            device_id=device, device_id_type=pl.DeviceIdType.MESH,
        )

    def send(src, dst, ssem, rsem, device):
        copy = remote(src, dst, ssem, rsem, device)
        copy.start()
        pending.append(copy)

    def arrived(dst, ssem, rsem, device):
        remote(dst, dst, ssem, rsem, device).wait_recv()

    class Gather:
        def __init__(self, n, at, me, view, ssem, rsem, absolute=False):
            self.n, self.at, self.me, self.view = n, at, me, view
            self.ssem, self.rsem, self.absolute = ssem, rsem, absolute

        def send(self, way, half, step):
            sign = 1 - 2 * way
            src = self.view((-sign * (step - 1)) % self.n, half)
            dst = src if self.absolute else self.view((-sign * step) % self.n, half)
            k = (way, half, step - 1)
            send(src, dst, self.ssem.at[k], self.rsem.at[k], self.at(self.me + sign))

        def start(self):
            for way in range(2):
                for half in (way, 1 - way):
                    if hops(self.n, way, half) >= 1:
                        self.send(way, half, 1)

        def step(self, step, after=None):
            for half in range(2):
                for way in range(2):
                    if hops(self.n, way, half) >= step:
                        sign = 1 - 2 * way
                        off = (-sign * step) % self.n
                        k = (way, half, step - 1)
                        arrived(self.view(off, half), self.ssem.at[k], self.rsem.at[k],
                                self.at(self.me + sign))
                        if hops(self.n, way, half) >= step + 1:
                            self.send(way, half, step + 1)
                        if after is not None:
                            after(off, half)

    class Scatter:
        def __init__(self, n, at, me, part, sbuf, rbuf, ssem, rsem):
            self.n, self.at, self.me, self.part = n, at, me, part
            self.sbuf, self.rbuf, self.ssem, self.rsem = sbuf, rbuf, ssem, rsem

        def wait(self, way, half, i):
            k = (way, half, i)
            arrived(self.rbuf.at[k], self.ssem.at[k], self.rsem.at[k],
                    self.at(self.me + 1 - 2 * way))

        def step(self, i):
            for half in range(2):
                for way in range(2):
                    length = hops(self.n, way, half)
                    if i >= length:
                        continue
                    sign = 1 - 2 * way
                    k = (way, half, i)
                    value = self.part[(sign * (length - i)) % self.n, half]
                    if i > 0:
                        self.wait(way, half, i - 1)
                        value = value + self.rbuf[way, half, i - 1].astype(F32)
                    self.sbuf[k] = value.astype(BF16)
                    send(self.sbuf.at[k], self.rbuf.at[k], self.ssem.at[k], self.rsem.at[k],
                         self.at(self.me + sign))

        def finish(self, half):
            value = self.part[0, half]
            for way in range(2):
                length = hops(self.n, way, half)
                if length >= 1:
                    self.wait(way, half, length - 1)
                    value = value + self.rbuf[way, half, length - 1].astype(F32)
            return value

    own_w = pltpu.make_async_copy(w.at[x], Wb.at[0], loc.at[0])
    own_w.start()
    own_a = pltpu.make_async_copy(pairs.at[:, :, z, d], S1.at[pl.ds(2 * z, 2)], loc.at[1])
    own_a.start()
    T[0] = tok[...]
    C[0] = cot[...]

    barrier = pltpu.get_barrier_semaphore()
    partners = (
        [at_z(z + m) for m in range(1, nz)]
        + [at_x(x + m) for m in range(1, nx)]
        + [at_dp(d + m) for m in range(1, nd)]
    )
    for device in partners:
        pl.semaphore_signal(barrier, inc=1, device_id=device, device_id_type=pl.DeviceIdType.MESH)
    pl.semaphore_wait(barrier, len(partners))

    gather_t = Gather(nz, at_z, z, lambda off, h: T.at[off, h], t_s, t_r)
    gather_c = Gather(nx, at_x, x, lambda off, h: C.at[off, h], c_s, c_r)
    gather_w = Gather(
        ny, at_y, y,
        lambda off, h: Wb.at[pl.ds(1, nx - 1), lax.rem(y + off, ny) * CORES + c, h],
        wy_s, wy_r, absolute=True,
    )
    gather_g = Gather(
        ny, at_y, y,
        lambda off, h: G.at[CORES * off, :, pl.ds(h * (feat // 2), feat // 2)], gy_s, gy_r,
    )
    scatter_z = Scatter(nz, at_z, z, Pz, zs, zr, rz_s, rz_r)
    scatter_x = Scatter(nx, at_x, x, acc, xs, xr, rx_s, rx_r)

    def w_piece(off, core, h):
        return Wb.at[pl.ds(1, nx - 1), lax.rem(y + off, ny) * CORES + core, h]

    def w_share(off, h):
        piece = w_piece(off, c, h)
        send(piece, piece, wc_s.at[off, h], wc_r.at[off, h], sibling)

    def g_piece(off, core, h):
        return G.at[CORES * off + core, :, pl.ds(h * (feat // 2), feat // 2)]

    def g_share(off, h):
        send(g_piece(off, 0, h), g_piece(off, 1, h), gc_s.at[off, h], gc_r.at[off, h], sibling)

    for k in range(1, nx):
        send(w.at[lax.rem(x - k + nx, nx), d], Wb.at[k, d], wx_s.at[k], wx_r.at[k], at_x(x - k))
    for m in range(1, nz):
        send(pairs.at[:, :, lax.rem(z + m, nz), d], S1.at[pl.ds(2 * z, 2)],
             a1_s.at[m], a1_r.at[m], at_z(z + m))
    gather_t.start()
    gather_c.start()

    for k in range(1, nx):
        arrived(Wb.at[k, d], wx_s.at[k], wx_r.at[k], at_x(x - k))
    gather_w.start()
    for h in range(2):
        w_share(0, h)
    gather_t.step(1)
    gather_c.step(1)

    own_a.wait()
    for m in range(1, nz):
        src = lax.rem(z - m + nz, nz)
        arrived(S1.at[pl.ds(2 * src, 2)], a1_s.at[m], a1_r.at[m], at_z(z + m))
    for k in range(1, nx):
        send(S1.at[:, lax.rem(x + k, nx)], S2.at[pl.ds(2 * nz * x, 2 * nz)],
             a2_s.at[k], a2_r.at[k], at_x(x + k))
    S2[pl.ds(2 * nz * x, 2 * nz)] = S1[:, x]
    gather_w.step(1, w_share)
    gather_t.step(2)
    for s in range(2, nx // 2 + 1):
        gather_c.step(s)
    for k in range(1, nx):
        src = lax.rem(x - k + nx, nx)
        arrived(S2.at[pl.ds(2 * nz * src, 2 * nz)], a2_s.at[k], a2_r.at[k], at_x(x + k))

    for m in range(nd):
        other = lax.rem(d + m, nd)
        for s in range(segs):
            sel[m, s] = S2[owner[seg[other, s]]]
        if m > 0:
            send(sel.at[m], R.at[:, d], a3_s.at[m], a3_r.at[m], at_dp(d + m))
    R[:, d] = sel[0]
    for s in range(2, ny // 2 + 1):
        gather_w.step(s, w_share)
    for m in range(1, nd):
        src = lax.rem(d - m + nd, nd)
        arrived(R.at[:, src], a3_s.at[m], a3_r.at[m], at_dp(d + m))

    row = lax.broadcasted_iota(jnp.int32, (rows, lanes), 0)
    lane = lax.broadcasted_iota(jnp.int32, (rows, lanes), 1)
    starts = [jnp.int32(0)]
    for s in range(segs):
        starts.append(starts[-1] + lens[0, s])

    def mask(s):
        return (row >= starts[s]) & (row < starts[s + 1])

    tok2 = tok[...].reshape(rows, feat)
    cot2 = cot[...].reshape(rows, feat)
    part = jnp.zeros((rows, lanes), F32)
    for s in range(segs):
        pair = R[s].reshape(feat, lanes)
        both = jnp.where(lane < rank, dot(tok2, pair), dot(cot2, pair))
        part = part + jnp.where(mask(s), both, 0.0)
    Lp[...] = part.reshape(Lp.shape)
    for k in range(1, nx):
        send(Lp.at[lax.rem(x + k, nx)], X1.at[k], l1_s.at[k], l1_r.at[k], at_x(x + k))

    own_w.wait()
    for off in range(ny):
        for h in range(2):
            arrived(w_piece(off, 1 - c, h), wc_s.at[off, h], wc_r.at[off, h], sibling)

    def partial_ig(off):
        tile = lax.rem(z + off, nz)
        total = jnp.zeros((rows, feat), F32)
        for k in range(nx):
            total = total + dot(C[k].reshape(rows, feat), Wb[k, tile].reshape(feat, feat), NT)
        Pz[off] = total.reshape(2, half_rows, feat)

    def far_body(i, carry):
        partial_ig(i + nz // 2 - 1)
        return carry

    lax.fori_loop(0, 3, far_body, 0)
    scatter_z.step(0)

    for k in range(1, nx):
        arrived(X1.at[k], l1_s.at[k], l1_r.at[k], at_x(x + k))
    total = Lp[x]
    for k in range(1, nx):
        total = total + X1[k]
    Lz[...] = total.reshape(Lz.shape)
    for m in range(1, nz):
        send(Lz.at[lax.rem(z + m, nz)], Z1.at[m], l2_s.at[m], l2_r.at[m], at_z(z + m))
    gather_t.step(3)

    def near_body(i, carry):
        partial_ig(lax.rem(i + nz // 2 + 2, nz))
        return carry

    lax.fori_loop(0, nz - 3, near_body, 0)

    for m in range(1, nz):
        arrived(Z1.at[m], l2_s.at[m], l2_r.at[m], at_z(z + m))
    total = Lz[z]
    for m in range(1, nz):
        total = total + Z1[m]
    Lf[x, z] = pltpu.roll(total, rank, 1).astype(BF16)
    for m in range(1, nz):
        send(Lf.at[x, z], Lf.at[x, z], l3_s.at[m], l3_r.at[m], at_z(z + m))
    scatter_z.step(1)

    def partial_out(m, first):
        tile = lax.rem(z + m, nz)
        block = T[m].reshape(rows, feat)

        def body(k, carry):
            value = dot(block, Wb[k, tile].reshape(feat, feat)).reshape(2, half_rows, feat)
            acc[k] = value if first else acc[k] + value
            return carry

        lax.fori_loop(0, nx, body, 0)

    partial_out(0, True)

    def near_out(i, carry):
        partial_out(lax.rem(jnp.where(i < 2, i + nz - 2, i - 1), nz), False)
        return carry

    near = 4 if nz > 4 else 2
    if nz > 4:
        lax.fori_loop(0, 4, near_out, 0)

    for m in range(1, nz):
        src = lax.rem(z - m + nz, nz)
        arrived(Lf.at[x, src], l3_s.at[m], l3_r.at[m], at_z(z + m))
    for k in range(1, nx):
        send(Lf.at[x], Lf.at[x], l4_s.at[k], l4_r.at[k], at_x(x + k))

    for s in range(4, nz // 2 + 1):
        gather_t.step(s)

    def far_out(i, carry):
        if nz > 4:
            partial_out(i + 3, False)
        else:
            partial_out(i + 1, False)
        return carry

    lax.fori_loop(0, nz - 5 if nz > 4 else nz - 1, far_out, 0)
    scatter_x.step(0)
    if nz // 2 > 2:
        scatter_z.step(2)

    for k in range(1, nx):
        src = lax.rem(x - k + nx, nx)
        arrived(Lf.at[src], l4_s.at[k], l4_r.at[k], at_x(x + k))
    both = Lf[...].reshape(rows, lanes)
    for s in range(segs):
        Lm[:, s * lanes:(s + 1) * lanes] = jnp.where(mask(s), both, jnp.zeros_like(both))
    g_tok = dot(tok2, Lm[...], TN)
    g_cot = dot(cot2, Lm[...], TN)
    g_lane = lax.broadcasted_iota(jnp.int32, (feat, lanes), 1)
    for s in range(segs):
        part_s = slice(s * lanes, (s + 1) * lanes)
        G[0, s] = jnp.where(g_lane < rank, g_tok[:, part_s], g_cot[:, part_s]).astype(BF16)
    gather_g.start()
    for h in range(2):
        g_share(0, h)

    fix_out = jnp.zeros((rows, feat), F32)
    fix_ig = jnp.zeros((rows, feat), F32)
    for s in range(segs):
        pair = R[s].reshape(feat, lanes)
        mine = Lm[:, s * lanes:(s + 1) * lanes]
        zero = jnp.zeros_like(mine)
        fix_out = fix_out + dot(jnp.where(lane < rank, zero, mine), pair, NT)
        fix_ig = fix_ig + dot(jnp.where(lane < rank, mine, zero), pair, NT)
    acc[0] = acc[0] + fix_out.reshape(2, half_rows, feat)
    Pz[0] = Pz[0] + fix_ig.reshape(2, half_rows, feat)

    for i in range(1, nx // 2):
        scatter_x.step(i)
    for i in range(3, nz // 2):
        scatter_z.step(i)
    gather_g.step(1, g_share)

    slots = grad.shape[0]
    chunk = min(32, feat)

    def add_grads(i, first):
        off, core = i // CORES, i % CORES
        src = lax.rem(y + off, ny) * CORES + jnp.where(core == 0, c, 1 - c)
        hit = [[(owner[seg[src, s]] == slots * d + q).astype(F32) for s in range(segs)]
               for q in range(slots)]

        def body(r, carry):
            at = pl.ds(pl.multiple_of(r * chunk, chunk), chunk)
            given = [G[i, s, at].astype(F32) for s in range(segs)]
            for q in range(slots):
                value = given[0] * hit[q][0]
                for s in range(1, segs):
                    value = value + given[s] * hit[q][s]
                grad[q, at] = value if first else grad[q, at] + value
            return carry

        lax.fori_loop(0, feat // chunk, body, 0)

    add_grads(0, True)

    for h in range(2):
        out[h] = scatter_x.finish(h).astype(BF16)

    def g_wait(off):
        for h in range(2):
            arrived(g_piece(off, 1, h), gc_s.at[off, h], gc_r.at[off, h], sibling)

    for s in range(2, ny // 2 + 1):
        gather_g.step(s, g_share)
    for off in range(ny):
        g_wait(off)

    def grads_body(i, carry):
        add_grads(i, False)
        return carry

    lax.fori_loop(1, nd, grads_body, 0)

    for h in range(2):
        ig[h] = scatter_z.finish(h).astype(BF16)

    for copy in pending:
        copy.wait_send()


def local(tokens, base_weight, adapter_pairs, owner_map, seg_adapter, seg_lengths, cotangent):
    rows, feat = tokens.shape
    half = rows // 2
    nz = NZ
    nx = lax.axis_size("mp") // nz
    ny = lax.axis_size("dp") // CORES
    nd = ny * CORES
    stored, depth, lanes = adapter_pairs.shape
    segs = seg_lengths.shape[1]
    total_slots = stored * nx * nz
    slots = total_slots // nd
    piece = feat // nd
    lrows = rows // (nx * nz)
    vmem = lambda shape, dtype: pltpu.VMEM(shape, dtype)
    dma = lambda *shape: pltpu.SemaphoreType.DMA(shape)
    ring = lambda n: [dma(2, 2, n // 2)] * 2
    pair = lambda *shape: [dma(*shape)] * 2
    scratch = [
        vmem((nz, 2, half, feat), BF16),
        vmem((nx, 2, half, feat), BF16),
        vmem((nx, nz, 2, feat // 2, feat), BF16),
        vmem((stored * nz, nx, piece, lanes), BF16),
        vmem((total_slots, piece, lanes), BF16),
        vmem((nd, segs, piece, lanes), BF16),
        vmem((segs, nd, piece, lanes), BF16),
        vmem((nx, rows // nx, lanes), F32),
        vmem((nx, rows // nx, lanes), F32),
        vmem((nz, lrows, lanes), F32),
        vmem((nz, lrows, lanes), F32),
        vmem((nx, nz, lrows, lanes), BF16),
        vmem((rows, segs * lanes), BF16),
        vmem((nx, 2, half, feat), F32),
        vmem((nz, 2, half, feat), F32),
        vmem((2, 2, nz // 2, half, feat), BF16),
        vmem((2, 2, nz // 2, half, feat), BF16),
        vmem((2, 2, nx // 2, half, feat), BF16),
        vmem((2, 2, nx // 2, half, feat), BF16),
        vmem((nd, segs, feat, lanes), BF16),
        *ring(nz), *ring(nx), *pair(nx), *ring(ny), *pair(ny, 2),
        *pair(nz), *pair(nx), *pair(nd),
        *pair(nx), *pair(nz), *pair(nz), *pair(nx),
        *ring(nz), *ring(nx), *ring(ny), *pair(ny, 2), dma(2),
    ]
    in_vmem = pl.BlockSpec(memory_space=pltpu.VMEM)
    in_smem = pl.BlockSpec(memory_space=pltpu.SMEM)
    in_any = pl.BlockSpec(memory_space=pl.ANY)
    out, ig, grad = pl.pallas_call(
        functools.partial(kernel, nx, nz, ny),
        out_shape=[
            jax.ShapeDtypeStruct((2, half, feat), BF16),
            jax.ShapeDtypeStruct((2, half, feat), BF16),
            jax.ShapeDtypeStruct((slots, feat, lanes), F32),
        ],
        in_specs=[in_vmem, in_vmem, in_any, in_any, in_smem, in_smem, in_smem],
        out_specs=[in_vmem] * 3,
        scratch_shapes=scratch,
        compiler_params=pltpu.CompilerParams(
            collective_id=0, has_side_effects=True, vmem_limit_bytes=56 * 1024 * 1024
        ),
    )(
        tokens.reshape(2, half, feat),
        cotangent.reshape(2, half, feat),
        base_weight.reshape(nx, nz, 2, feat // 2, feat),
        adapter_pairs.reshape(stored, nx, nz, nd, piece, lanes),
        owner_map,
        seg_adapter,
        seg_lengths,
    )
    return out.reshape(rows, feat), ig.reshape(rows, feat), grad


def solution(mesh):
    in_specs = (
        P("dp", "mp"),
        P(None, "mp"),
        P("mp", None, None),
        P(),
        P(),
        P("dp", None),
        P("dp", "mp"),
    )
    out_specs = (P("dp", "mp"), P("dp", "mp"), P("dp", "mp", None))
    return jax.shard_map(local, mesh=mesh, in_specs=in_specs, out_specs=out_specs, check_vma=False)
```

```python
import functools

import jax
import jax.numpy as jnp
from jax import lax
from jax.experimental import pallas as pl
from jax.experimental.pallas import tpu as pltpu
from jax.sharding import PartitionSpec as P

NZ = 8
CORES = 2
QT = 1
QI = 1
F32 = jnp.float32
BF16 = jnp.bfloat16
SCHEDULE = "WLTWCLWCTWTLCTTWWLCiiTooITLIoIoiTLoIOIOGiOISiGIFGSSOI"
NT = (((1,), (1,)), ((), ()))
TN = (((0,), (0,)), ((), ()))


def dot(a, b, dims=(((1,), (0,)), ((), ()))):
    return lax.dot_general(a, b, dims, preferred_element_type=F32)


def hops(n, way, half):
    return n // 2 if way == half else n // 2 - 1


def kernel(
    nx, nz, ny,
    tok, cot, w, pairs, owner, seg, lens,
    out, ig, grad,
    T, C, Wb, S2, sel, R, Lp, X1, Lz, Z1, Lf, Lm, acc, Pz, zs, zr, xs, xr, G,
    t_s, t_r, c_s, c_r, wx_s, wx_r, wy_s, wy_r, wc_s, wc_r,
    a1_s, a1_r, a3_s, a3_r, lx_s, lx_r, lz_s, lz_r, l2_s, l2_r,
    rz_s, rz_r, rx_s, rx_r, gy_s, gy_r, gc_s, gc_r, loc,
):
    nd = ny * CORES
    d = lax.axis_index("dp")
    j = lax.axis_index("mp")
    y, c = d // CORES, d % CORES
    x, z = j // nz, j % nz
    half_rows, feat = tok.shape[1], tok.shape[2]
    rows = 2 * half_rows
    lanes = 2 * (pairs.shape[-1] // 2)
    rank = lanes // 2
    segs = R.shape[0]
    sibling = (CORES * y + 1 - c, j)

    def at_x(r):
        return (d, lax.rem(r + nx, nx) * nz + z)

    def at_z(r):
        return (d, x * nz + lax.rem(r + nz, nz))

    def at_y(r):
        return (lax.rem(r + ny, ny) * CORES + c, j)

    def at_dp(r):
        return (lax.rem(r + nd, nd), j)

    pending = []

    def remote(src, dst, ssem, rsem, device):
        return pltpu.make_async_remote_copy(
            src_ref=src, dst_ref=dst, send_sem=ssem, recv_sem=rsem,
            device_id=device, device_id_type=pl.DeviceIdType.MESH,
        )

    def send(src, dst, ssem, rsem, device):
        copy = remote(src, dst, ssem, rsem, device)
        copy.start()
        pending.append(copy)

    def arrived(dst, ssem, rsem, device):
        remote(dst, dst, ssem, rsem, device).wait_recv()

    class Fan:
        def __init__(self, count, at, src, dst, landed, ssem, rsem):
            self.count, self.at, self.src, self.dst, self.landed = count, at, src, dst, landed
            self.ssem, self.rsem = ssem, rsem

        def start(self):
            for m in range(1, self.count):
                send(self.src(m), self.dst(m), self.ssem.at[m], self.rsem.at[m], self.at(m))

        def wait(self):
            for m in range(1, self.count):
                arrived(self.landed(m), self.ssem.at[m], self.rsem.at[m], self.at(m))

    class Gather:
        def __init__(self, n, at, me, view, ssem, rsem, absolute=False):
            self.n, self.at, self.me, self.view = n, at, me, view
            self.ssem, self.rsem, self.absolute = ssem, rsem, absolute
            self.pieces = ssem.shape[2]

        def send(self, way, half, piece, step):
            sign = 1 - 2 * way
            src = self.view((-sign * (step - 1)) % self.n, half, piece)
            dst = src if self.absolute else self.view((-sign * step) % self.n, half, piece)
            k = (way, half, piece, step - 1)
            send(src, dst, self.ssem.at[k], self.rsem.at[k], self.at(self.me + sign))

        def start(self):
            for turn in range(2):
                for piece in range(self.pieces):
                    for way in range(2):
                        half = way if turn == 0 else 1 - way
                        if hops(self.n, way, half) >= 1:
                            self.send(way, half, piece, 1)

        def turns(self, step):
            return [turn for turn in range(2) if hops(self.n, 0, turn) >= step]

        def step(self, step, turn, after=None):
            for piece in range(self.pieces):
                for way in range(2):
                    half = way if turn == 0 else 1 - way
                    sign = 1 - 2 * way
                    off = (-sign * step) % self.n
                    k = (way, half, piece, step - 1)
                    arrived(self.view(off, half, piece), self.ssem.at[k], self.rsem.at[k],
                            self.at(self.me + sign))
                    if hops(self.n, way, half) >= step + 1:
                        self.send(way, half, piece, step + 1)
                    if after is not None:
                        after(off, half)

        def steps(self, after=None):
            self.start()
            yield
            for step in range(1, self.n // 2 + 1):
                for turn in self.turns(step):
                    self.step(step, turn, after)
                    yield

    class Scatter:
        def __init__(self, n, at, me, part, sbuf, rbuf, ssem, rsem):
            self.n, self.at, self.me, self.part = n, at, me, part
            self.sbuf, self.rbuf, self.ssem, self.rsem = sbuf, rbuf, ssem, rsem
            self.pieces = ssem.shape[2]
            self.size = part.shape[2] // self.pieces

        def rows(self, piece):
            return pl.ds(piece * self.size, self.size)

        def wait(self, way, half, piece, i):
            k = (way, half, piece, i)
            arrived(self.rbuf.at[way, half, i, self.rows(piece)], self.ssem.at[k],
                    self.rsem.at[k], self.at(self.me + 1 - 2 * way))

        def step(self, i, turn):
            for piece in range(self.pieces):
                for way in range(2):
                    half = way if turn == 0 else 1 - way
                    length = hops(self.n, way, half)
                    sign = 1 - 2 * way
                    k = (way, half, piece, i)
                    at = self.rows(piece)
                    value = self.part[(sign * (length - i)) % self.n, half, at]
                    if i > 0:
                        self.wait(way, half, piece, i - 1)
                        value = value + self.rbuf[way, half, i - 1, at].astype(F32)
                    self.sbuf[way, half, i, at] = value.astype(BF16)
                    send(self.sbuf.at[way, half, i, at], self.rbuf.at[way, half, i, at],
                         self.ssem.at[k], self.rsem.at[k], self.at(self.me + sign))

        def steps(self, result):
            for i in range(self.n // 2):
                for turn in range(2):
                    if i < hops(self.n, 0, turn):
                        self.step(i, turn)
                        yield
            for half in range(2):
                for piece in range(self.pieces):
                    result[half, self.rows(piece)] = self.finish(half, piece)
            yield

        def finish(self, half, piece):
            at = self.rows(piece)
            value = self.part[0, half, at]
            for way in range(2):
                length = hops(self.n, way, half)
                if length >= 1:
                    self.wait(way, half, piece, length - 1)
                    value = value + self.rbuf[way, half, length - 1, at].astype(F32)
            return value.astype(BF16)

    row = lax.broadcasted_iota(jnp.int32, (rows, lanes), 0)
    lane = lax.broadcasted_iota(jnp.int32, (rows, lanes), 1)
    starts = [jnp.int32(0)]
    for s in range(segs):
        starts.append(starts[-1] + lens[0, s])

    def mask(s):
        return (row >= starts[s]) & (row < starts[s + 1])

    t_size = half_rows // t_s.shape[2]
    gather_t = Gather(nz, at_z, z, lambda off, h, q: T.at[off, h, pl.ds(q * t_size, t_size)], t_s, t_r)
    gather_c = Gather(nx, at_x, x, lambda off, h, q: C.at[off, h], c_s, c_r)

    def w_piece(off, core, h):
        return Wb.at[pl.ds(1, nx - 1), lax.rem(y + off, ny) * CORES + core, h]

    def g_piece(off, core, h):
        return G.at[CORES * off + core, :, pl.ds(h * (feat // 2), feat // 2)]

    gather_w = Gather(ny, at_y, y, lambda off, h, q: w_piece(off, c, h), wy_s, wy_r, absolute=True)
    gather_g = Gather(ny, at_y, y, lambda off, h, q: g_piece(off, 0, h), gy_s, gy_r)
    scatter_z = Scatter(nz, at_z, z, Pz, zs, zr, rz_s, rz_r)
    scatter_x = Scatter(nx, at_x, x, acc, xs, xr, rx_s, rx_r)

    def w_share(off, h):
        piece = w_piece(off, c, h)
        send(piece, piece, wc_s.at[off, h], wc_r.at[off, h], sibling)

    def g_share(off, h):
        send(g_piece(off, 0, h), g_piece(off, 1, h), gc_s.at[off, h], gc_r.at[off, h], sibling)

    def at_mp(m):
        return (d, lax.rem(x + m // nz, nx) * nz + lax.rem(z + m % nz, nz))

    def from_mp(m):
        return lax.rem(x - m // nz + nx, nx) * nz + lax.rem(z - m % nz + nz, nz)

    fan_a = Fan(
        nx * nz, at_mp,
        lambda m: pairs.at[:, lax.rem(x + m // nz, nx), lax.rem(z + m % nz, nz), d],
        lambda m: S2.at[pl.ds(2 * j, 2)],
        lambda m: S2.at[pl.ds(2 * from_mp(m), 2)], a1_s, a1_r,
    )
    fan_r = Fan(
        nd, lambda m: at_dp(d + m), lambda m: sel.at[m], lambda m: R.at[:, d],
        lambda m: R.at[:, lax.rem(d - m + nd, nd)], a3_s, a3_r,
    )
    fan_lx = Fan(
        nx, lambda k: at_x(x + k), lambda k: Lp.at[lax.rem(x + k, nx)], lambda k: X1.at[k],
        lambda k: X1.at[k], lx_s, lx_r,
    )
    fan_lz = Fan(
        nz, lambda m: at_z(z + m), lambda m: Lz.at[lax.rem(z + m, nz)], lambda m: Z1.at[m],
        lambda m: Z1.at[m], lz_s, lz_r,
    )
    fan_f = Fan(
        nx * nz, at_mp, lambda m: Lf.at[j], lambda m: Lf.at[j], lambda m: Lf.at[from_mp(m)],
        l2_s, l2_r,
    )
    own_w = pltpu.make_async_copy(w.at[x], Wb.at[0], loc.at[0])
    own_a = pltpu.make_async_copy(pairs.at[:, x, z, d], S2.at[pl.ds(2 * j, 2)], loc.at[1])

    def weights():
        for k in range(1, nx):
            send(w.at[lax.rem(x - k + nx, nx), d], Wb.at[k, d], wx_s.at[k], wx_r.at[k], at_x(x - k))
        yield
        for k in range(1, nx):
            arrived(Wb.at[k, d], wx_s.at[k], wx_r.at[k], at_x(x - k))
        steps = gather_w.steps(w_share)
        next(steps)
        for h in range(2):
            w_share(0, h)
        yield
        yield from steps
        own_w.wait()
        for off in range(ny):
            for h in range(2):
                arrived(w_piece(off, 1 - c, h), wc_s.at[off, h], wc_r.at[off, h], sibling)
        yield

    grads = gather_g.steps(g_share)

    def lora():
        fan_a.start()
        yield
        own_a.wait()
        fan_a.wait()
        for m in range(nd):
            other = lax.rem(d + m, nd)
            for s in range(segs):
                sel[m, s] = S2[owner[seg[s, other]]]
        fan_r.start()
        R[:, d] = sel[0]
        yield
        fan_r.wait()
        tok2 = tok[...].reshape(rows, feat)
        cot2 = cot[...].reshape(rows, feat)
        part = jnp.zeros((rows, lanes), F32)
        for s in range(segs):
            pair = R[s].reshape(feat, lanes)
            both = jnp.where(lane < rank, dot(tok2, pair), dot(cot2, pair))
            part = part + jnp.where(mask(s), both, 0.0)
        Lp[...] = part.reshape(Lp.shape)
        fan_lx.start()
        yield
        fan_lx.wait()
        total = Lp[x]
        for k in range(1, nx):
            total = total + X1[k]
        Lz[...] = total.reshape(Lz.shape)
        fan_lz.start()
        yield
        fan_lz.wait()
        total = Lz[z]
        for m in range(1, nz):
            total = total + Z1[m]
        Lf[j] = pltpu.roll(total, rank, 1).astype(BF16)
        fan_f.start()
        yield
        fan_f.wait()
        both = Lf[...].reshape(rows, lanes)
        for s in range(segs):
            Lm[:, s * lanes:(s + 1) * lanes] = jnp.where(mask(s), both, jnp.zeros_like(both))
        g_tok = dot(tok[...].reshape(rows, feat), Lm[...], TN)
        g_cot = dot(cot[...].reshape(rows, feat), Lm[...], TN)
        g_lane = lax.broadcasted_iota(jnp.int32, (feat, lanes), 1)
        for s in range(segs):
            part_s = slice(s * lanes, (s + 1) * lanes)
            G[0, s] = jnp.where(g_lane < rank, g_tok[:, part_s], g_cot[:, part_s]).astype(BF16)
        next(grads)
        for h in range(2):
            g_share(0, h)
        yield

    def fix():
        fix_out = jnp.zeros((rows, feat), F32)
        fix_ig = jnp.zeros((rows, feat), F32)
        for s in range(segs):
            pair = R[s].reshape(feat, lanes)
            mine = Lm[:, s * lanes:(s + 1) * lanes]
            zero = jnp.zeros_like(mine)
            fix_out = fix_out + dot(jnp.where(lane < rank, zero, mine), pair, NT)
            fix_ig = fix_ig + dot(jnp.where(lane < rank, mine, zero), pair, NT)
        acc[0] = acc[0] + fix_out.reshape(2, half_rows, feat)
        Pz[0] = Pz[0] + fix_ig.reshape(2, half_rows, feat)
        yield

    slots = grad.shape[0]
    chunk = min(32, feat)

    def add_grads(i, first):
        off, core = i // CORES, i % CORES
        src = lax.rem(y + off, ny) * CORES + jnp.where(core == 0, c, 1 - c)
        hit = [[(owner[seg[s, src]] == slots * d + q).astype(F32) for s in range(segs)]
               for q in range(slots)]

        def body(r, carry):
            at = pl.ds(pl.multiple_of(r * chunk, chunk), chunk)
            given = [G[i, s, at].astype(F32) for s in range(segs)]
            for q in range(slots):
                value = given[0] * hit[q][0]
                for s in range(1, segs):
                    value = value + given[s] * hit[q][s]
                grad[q, at] = value if first else grad[q, at] + value
            return carry

        lax.fori_loop(0, feat // chunk, body, 0)

    def slots_grad():
        def add(first, count, stride):
            def body(i, carry):
                add_grads(first + i * stride, False)
                return carry

            lax.fori_loop(0, count, body, 0)

        def shared(off):
            for h in range(2):
                arrived(g_piece(off, 1, h), gc_s.at[off, h], gc_r.at[off, h], sibling)

        add_grads(0, True)
        shared(0)
        add(1, 1, 1)
        yield
        if ny > 2:
            add(CORES, 2, CORES * (ny - 2))
            yield
        add(ny, 1, 1)
        for off in range(1, ny):
            shared(off)
        add(CORES + 1, ny - 1, CORES)
        yield

    def partial_ig(off):
        tile = lax.rem(z + off, nz)
        total = jnp.zeros((rows, feat), F32)
        for k in range(nx):
            total = total + dot(C[k].reshape(rows, feat), Wb[k, tile].reshape(feat, feat), NT)
        Pz[off] = total.reshape(2, half_rows, feat)

    def igs():
        def ways(m):
            def body(i, carry):
                partial_ig(m + i * (nz - 2 * m))
                return carry

            lax.fori_loop(0, 2, body, 0)

        partial_ig(nz // 2)
        yield
        for m in range(nz // 2 - 1, 0, -1):
            ways(m)
            yield
        partial_ig(0)
        yield

    def partial_out(m, first):
        tile = lax.rem(z + m, nz)
        block = T[m].reshape(rows, feat)

        def body(k, carry):
            value = dot(block, Wb[k, tile].reshape(feat, feat)).reshape(2, half_rows, feat)
            acc[k] = value if first else acc[k] + value
            return carry

        lax.fori_loop(0, nx, body, 0)

    def outs():
        def ways(m):
            def body(i, carry):
                partial_out(m + i * (nz - 2 * m), False)
                return carry

            lax.fori_loop(0, 2, body, 0)

        partial_out(0, True)
        yield
        for m in range(1, nz // 2):
            ways(m)
            yield
        partial_out(nz // 2, False)
        yield

    own_w.start()
    own_a.start()
    T[0] = tok[...]
    C[0] = cot[...]

    barrier = pltpu.get_barrier_semaphore()
    partners = (
        [at_mp(m) for m in range(1, nx * nz)]
        + [at_dp(d + m) for m in range(1, nd)]
    )
    for device in partners:
        pl.semaphore_signal(barrier, inc=1, device_id=device, device_id_type=pl.DeviceIdType.MESH)
    pl.semaphore_wait(barrier, len(partners))

    tasks = {
        "W": weights(), "T": gather_t.steps(), "C": gather_c.steps(), "L": lora(), "F": fix(), "G": grads,
        "S": slots_grad(), "i": igs(), "I": scatter_z.steps(ig), "o": outs(), "O": scatter_x.steps(out),
    }
    for name in SCHEDULE:
        next(tasks[name], None)
    for task in tasks.values():
        for _ in task:
            pass

    for copy in pending:
        copy.wait_send()


def local(tokens, base_weight, adapter_pairs, owner_map, seg_adapter, seg_lengths, cotangent):
    rows, feat = tokens.shape
    half = rows // 2
    nz = NZ
    nx = lax.axis_size("mp") // nz
    ny = lax.axis_size("dp") // CORES
    nd = ny * CORES
    stored, depth, lanes = adapter_pairs.shape
    segs = seg_lengths.shape[1]
    total_slots = stored * nx * nz
    slots = total_slots // nd
    piece = feat // nd
    lrows = rows // (nx * nz)
    vmem = lambda shape, dtype: pltpu.VMEM(shape, dtype)
    dma = lambda *shape: pltpu.SemaphoreType.DMA(shape)
    ring = lambda n, pieces=1: [dma(2, 2, pieces, n // 2)] * 2
    pair = lambda *shape: [dma(*shape)] * 2
    scratch = [
        vmem((nz, 2, half, feat), BF16),
        vmem((nx, 2, half, feat), BF16),
        vmem((nx, nz, 2, feat // 2, feat), BF16),
        vmem((total_slots, piece, lanes), BF16),
        vmem((nd, segs, piece, lanes), BF16),
        vmem((segs, nd, piece, lanes), BF16),
        vmem((nx, rows // nx, lanes), F32),
        vmem((nx, rows // nx, lanes), F32),
        vmem((nz, lrows, lanes), F32),
        vmem((nz, lrows, lanes), F32),
        vmem((nx * nz, lrows, lanes), BF16),
        vmem((rows, segs * lanes), BF16),
        vmem((nx, 2, half, feat), F32),
        vmem((nz, 2, half, feat), F32),
        vmem((2, 2, nz // 2, half, feat), BF16),
        vmem((2, 2, nz // 2, half, feat), BF16),
        vmem((2, 2, nx // 2, half, feat), BF16),
        vmem((2, 2, nx // 2, half, feat), BF16),
        vmem((nd, segs, feat, lanes), BF16),
        *ring(nz, QT), *ring(nx), *pair(nx), *ring(ny), *pair(ny, 2),
        *pair(nx * nz), *pair(nd), *pair(nx), *pair(nz), *pair(nx * nz),
        *ring(nz, QI), *ring(nx), *ring(ny), *pair(ny, 2), dma(2),
    ]
    in_vmem = pl.BlockSpec(memory_space=pltpu.VMEM)
    in_smem = pl.BlockSpec(memory_space=pltpu.SMEM)
    in_any = pl.BlockSpec(memory_space=pl.ANY)
    out, ig, grad = pl.pallas_call(
        functools.partial(kernel, nx, nz, ny),
        out_shape=[
            pltpu.VMEM((2, half, feat), BF16),
            pltpu.VMEM((2, half, feat), BF16),
            pltpu.VMEM((slots, feat, lanes), F32),
        ],
        in_specs=[in_vmem, in_vmem, in_any, in_any, in_smem, in_smem, in_smem],
        out_specs=[in_vmem] * 3,
        scratch_shapes=scratch,
        compiler_params=pltpu.CompilerParams(
            collective_id=0, has_side_effects=True, vmem_limit_bytes=56 * 1024 * 1024
        ),
    )(
        tokens.reshape(2, half, feat),
        cotangent.reshape(2, half, feat),
        base_weight.reshape(nx, nz, 2, feat // 2, feat),
        adapter_pairs.reshape(stored, nx, nz, nd, piece, lanes),
        owner_map,
        seg_adapter.T,
        seg_lengths,
    )
    return out.reshape(rows, feat), ig.reshape(rows, feat), grad


def solution(mesh):
    in_specs = (
        P("dp", "mp"),
        P(None, "mp"),
        P("mp", None, None),
        P(),
        P(),
        P("dp", None),
        P("dp", "mp"),
    )
    out_specs = (P("dp", "mp"), P("dp", "mp"), P("dp", "mp", None))
    return jax.shard_map(local, mesh=mesh, in_specs=in_specs, out_specs=out_specs, check_vma=False)
```

```python
import functools

import jax
import jax.numpy as jnp
from jax import lax
from jax.experimental import pallas as pl
from jax.experimental.pallas import tpu as pltpu
from jax.sharding import PartitionSpec as P

NZ = 8
CORES = 2
QT = 1
QI = 1
F32 = jnp.float32
BF16 = jnp.bfloat16
SCHEDULE = "LTWCLCWTCLTTWLTLCWTWLWiIiIooToILiITooOIOiiSGIOGISGFSOI"
NT = (((1,), (1,)), ((), ()))
TN = (((0,), (0,)), ((), ()))


def dot(a, b, dims=(((1,), (0,)), ((), ()))):
    return lax.dot_general(a, b, dims, preferred_element_type=F32)


def hops(n, way, half):
    return n // 2 if way == half else n // 2 - 1


def kernel(
    nx, nz, ny,
    tok, cot, w, pairs, owner, seg, lens,
    out, ig, grad,
    T, C, Wb, S2, sel, R, Lp, X1, Lz, Z1, Lf, Lm, acc, Pz, zs, zr, xs, xr, G,
    t_s, t_r, c_s, c_r, wx_s, wx_r, wy_s, wy_r, wc_s, wc_r,
    a1_s, a1_r, a3_s, a3_r, lx_s, lx_r, lz_s, lz_r, fz_s, fz_r, fx_s, fx_r,
    rz_s, rz_r, rx_s, rx_r, gy_s, gy_r, gc_s, gc_r, loc,
):
    nd = ny * CORES
    d = lax.axis_index("dp")
    j = lax.axis_index("mp")
    y, c = d // CORES, d % CORES
    x, z = j // nz, j % nz
    half_rows, feat = tok.shape[1], tok.shape[2]
    rows = 2 * half_rows
    lanes = 2 * (pairs.shape[-1] // 2)
    rank = lanes // 2
    segs = R.shape[0]
    sibling = (CORES * y + 1 - c, j)

    def at_x(r):
        return (d, lax.rem(r + nx, nx) * nz + z)

    def at_z(r):
        return (d, x * nz + lax.rem(r + nz, nz))

    def at_y(r):
        return (lax.rem(r + ny, ny) * CORES + c, j)

    def at_dp(r):
        return (lax.rem(r + nd, nd), j)

    pending = []

    def remote(src, dst, ssem, rsem, device):
        return pltpu.make_async_remote_copy(
            src_ref=src, dst_ref=dst, send_sem=ssem, recv_sem=rsem,
            device_id=device, device_id_type=pl.DeviceIdType.MESH,
        )

    def send(src, dst, ssem, rsem, device):
        copy = remote(src, dst, ssem, rsem, device)
        copy.start()
        pending.append(copy)

    def arrived(dst, ssem, rsem, device):
        remote(dst, dst, ssem, rsem, device).wait_recv()

    class Fan:
        def __init__(self, count, at, src, dst, landed, ssem, rsem):
            self.count, self.at, self.src, self.dst, self.landed = count, at, src, dst, landed
            self.ssem, self.rsem = ssem, rsem

        def start(self):
            for m in range(1, self.count):
                send(self.src(m), self.dst(m), self.ssem.at[m], self.rsem.at[m], self.at(m))

        def wait(self):
            for m in range(1, self.count):
                arrived(self.landed(m), self.ssem.at[m], self.rsem.at[m], self.at(m))

    class Gather:
        def __init__(self, n, at, me, view, ssem, rsem, absolute=False):
            self.n, self.at, self.me, self.view = n, at, me, view
            self.ssem, self.rsem, self.absolute = ssem, rsem, absolute
            self.pieces = ssem.shape[2]

        def send(self, way, half, piece, step):
            sign = 1 - 2 * way
            src = self.view((-sign * (step - 1)) % self.n, half, piece)
            dst = src if self.absolute else self.view((-sign * step) % self.n, half, piece)
            k = (way, half, piece, step - 1)
            send(src, dst, self.ssem.at[k], self.rsem.at[k], self.at(self.me + sign))

        def start(self):
            for turn in range(2):
                for piece in range(self.pieces):
                    for way in range(2):
                        half = way if turn == 0 else 1 - way
                        if hops(self.n, way, half) >= 1:
                            self.send(way, half, piece, 1)

        def turns(self, step):
            return [turn for turn in range(2) if hops(self.n, 0, turn) >= step]

        def step(self, step, turn, after=None):
            for piece in range(self.pieces):
                for way in range(2):
                    half = way if turn == 0 else 1 - way
                    sign = 1 - 2 * way
                    off = (-sign * step) % self.n
                    k = (way, half, piece, step - 1)
                    arrived(self.view(off, half, piece), self.ssem.at[k], self.rsem.at[k],
                            self.at(self.me + sign))
                    if hops(self.n, way, half) >= step + 1:
                        self.send(way, half, piece, step + 1)
                    if after is not None:
                        after(off, half)

        def steps(self, after=None):
            self.start()
            yield
            for step in range(1, self.n // 2 + 1):
                for turn in self.turns(step):
                    self.step(step, turn, after)
                    yield

    class Scatter:
        def __init__(self, n, at, me, part, sbuf, rbuf, ssem, rsem):
            self.n, self.at, self.me, self.part = n, at, me, part
            self.sbuf, self.rbuf, self.ssem, self.rsem = sbuf, rbuf, ssem, rsem
            self.pieces = ssem.shape[2]
            self.size = part.shape[2] // self.pieces

        def rows(self, piece):
            return pl.ds(piece * self.size, self.size)

        def wait(self, way, half, piece, i):
            k = (way, half, piece, i)
            arrived(self.rbuf.at[way, half, i, self.rows(piece)], self.ssem.at[k],
                    self.rsem.at[k], self.at(self.me + 1 - 2 * way))

        def step(self, i, turn):
            for piece in range(self.pieces):
                for way in range(2):
                    half = way if turn == 0 else 1 - way
                    length = hops(self.n, way, half)
                    sign = 1 - 2 * way
                    k = (way, half, piece, i)
                    at = self.rows(piece)
                    value = self.part[(sign * (length - i)) % self.n, half, at]
                    if i > 0:
                        self.wait(way, half, piece, i - 1)
                        value = value + self.rbuf[way, half, i - 1, at].astype(F32)
                    self.sbuf[way, half, i, at] = value.astype(BF16)
                    send(self.sbuf.at[way, half, i, at], self.rbuf.at[way, half, i, at],
                         self.ssem.at[k], self.rsem.at[k], self.at(self.me + sign))

        def steps(self, result):
            for i in range(self.n // 2):
                for turn in range(2):
                    if i < hops(self.n, 0, turn):
                        self.step(i, turn)
                        yield
            for half in range(2):
                for piece in range(self.pieces):
                    result[half, self.rows(piece)] = self.finish(half, piece)
            yield

        def finish(self, half, piece):
            at = self.rows(piece)
            value = self.part[0, half, at]
            for way in range(2):
                length = hops(self.n, way, half)
                if length >= 1:
                    self.wait(way, half, piece, length - 1)
                    value = value + self.rbuf[way, half, length - 1, at].astype(F32)
            return value.astype(BF16)

    row = lax.broadcasted_iota(jnp.int32, (rows, lanes), 0)
    lane = lax.broadcasted_iota(jnp.int32, (rows, lanes), 1)
    starts = [jnp.int32(0)]
    for s in range(segs):
        starts.append(starts[-1] + lens[0, s])

    def mask(s):
        return (row >= starts[s]) & (row < starts[s + 1])

    t_size = half_rows // t_s.shape[2]
    gather_t = Gather(nz, at_z, z, lambda off, h, q: T.at[off, h, pl.ds(q * t_size, t_size)], t_s, t_r)
    gather_c = Gather(nx, at_x, x, lambda off, h, q: C.at[off, h], c_s, c_r)

    def w_piece(off, core, h):
        return Wb.at[pl.ds(1, nx - 1), lax.rem(y + off, ny) * CORES + core, h]

    def g_piece(off, core, h):
        return G.at[CORES * off + core, :, pl.ds(h * (feat // 2), feat // 2)]

    gather_w = Gather(ny, at_y, y, lambda off, h, q: w_piece(off, c, h), wy_s, wy_r, absolute=True)
    gather_g = Gather(ny, at_y, y, lambda off, h, q: g_piece(off, 0, h), gy_s, gy_r)
    scatter_z = Scatter(nz, at_z, z, Pz, zs, zr, rz_s, rz_r)
    scatter_x = Scatter(nx, at_x, x, acc, xs, xr, rx_s, rx_r)

    def w_share(off, h):
        piece = w_piece(off, c, h)
        send(piece, piece, wc_s.at[off, h], wc_r.at[off, h], sibling)

    def g_share(off, h):
        send(g_piece(off, 0, h), g_piece(off, 1, h), gc_s.at[off, h], gc_r.at[off, h], sibling)

    def at_mp(m):
        return (d, lax.rem(x + m // nz, nx) * nz + lax.rem(z + m % nz, nz))

    def from_mp(m):
        return lax.rem(x - m // nz + nx, nx) * nz + lax.rem(z - m % nz + nz, nz)

    fan_a = Fan(
        nx * nz, at_mp,
        lambda m: pairs.at[:, lax.rem(x + m // nz, nx), lax.rem(z + m % nz, nz), d],
        lambda m: S2.at[pl.ds(2 * j, 2)],
        lambda m: S2.at[pl.ds(2 * from_mp(m), 2)], a1_s, a1_r,
    )
    fan_r = Fan(
        nd, lambda m: at_dp(d + m), lambda m: sel.at[m], lambda m: R.at[:, d],
        lambda m: R.at[:, lax.rem(d - m + nd, nd)], a3_s, a3_r,
    )
    fan_lx = Fan(
        nx, lambda k: at_x(x + k), lambda k: Lp.at[lax.rem(x + k, nx)], lambda k: X1.at[k],
        lambda k: X1.at[k], lx_s, lx_r,
    )
    fan_lz = Fan(
        nz, lambda m: at_z(z + m), lambda m: Lz.at[lax.rem(z + m, nz)], lambda m: Z1.at[m],
        lambda m: Z1.at[m], lz_s, lz_r,
    )
    fan_fz = Fan(
        nz, lambda m: at_z(z + m), lambda m: Lf.at[x, z], lambda m: Lf.at[x, z],
        lambda m: Lf.at[x, lax.rem(z - m + nz, nz)], fz_s, fz_r,
    )
    fan_fx = Fan(
        nx, lambda k: at_x(x + k), lambda k: Lf.at[x], lambda k: Lf.at[x],
        lambda k: Lf.at[lax.rem(x - k + nx, nx)], fx_s, fx_r,
    )
    own_t = pltpu.make_async_copy(tok, T.at[0], loc.at[2])
    own_c = pltpu.make_async_copy(cot, C.at[0], loc.at[3])
    own_w = pltpu.make_async_copy(w.at[x], Wb.at[0], loc.at[0])
    own_a = pltpu.make_async_copy(pairs.at[:, x, z, d], S2.at[pl.ds(2 * j, 2)], loc.at[1])

    def weights():
        for k in range(1, nx):
            send(w.at[lax.rem(x - k + nx, nx), d], Wb.at[k, d], wx_s.at[k], wx_r.at[k], at_x(x - k))
        yield
        for k in range(1, nx):
            arrived(Wb.at[k, d], wx_s.at[k], wx_r.at[k], at_x(x - k))
        steps = gather_w.steps(w_share)
        next(steps)
        for h in range(2):
            w_share(0, h)
        yield
        yield from steps
        own_w.wait()
        for off in range(ny):
            for h in range(2):
                arrived(w_piece(off, 1 - c, h), wc_s.at[off, h], wc_r.at[off, h], sibling)
        yield

    grads = gather_g.steps(g_share)

    def lora():
        fan_a.start()
        yield
        own_a.wait()
        fan_a.wait()
        for m in range(nd):
            other = lax.rem(d + m, nd)
            for s in range(segs):
                sel[m, s] = S2[owner[seg[s, other]]]
        fan_r.start()
        R[:, d] = sel[0]
        yield
        fan_r.wait()
        tok2 = T[0].reshape(rows, feat)
        cot2 = C[0].reshape(rows, feat)
        part = jnp.zeros((rows, lanes), F32)
        for s in range(segs):
            pair = R[s].reshape(feat, lanes)
            both = jnp.where(lane < rank, dot(tok2, pair), dot(cot2, pair))
            part = part + jnp.where(mask(s), both, 0.0)
        Lp[...] = part.reshape(Lp.shape)
        fan_lx.start()
        yield
        fan_lx.wait()
        total = Lp[x]
        for k in range(1, nx):
            total = total + X1[k]
        Lz[...] = total.reshape(Lz.shape)
        fan_lz.start()
        yield
        fan_lz.wait()
        total = Lz[z]
        for m in range(1, nz):
            total = total + Z1[m]
        Lf[x, z] = pltpu.roll(total, rank, 1).astype(BF16)
        fan_fz.start()
        yield
        fan_fz.wait()
        fan_fx.start()
        yield
        fan_fx.wait()
        both = Lf[...].reshape(rows, lanes)
        for s in range(segs):
            Lm[:, s * lanes:(s + 1) * lanes] = jnp.where(mask(s), both, jnp.zeros_like(both))
        g_tok = dot(T[0].reshape(rows, feat), Lm[...], TN)
        g_cot = dot(C[0].reshape(rows, feat), Lm[...], TN)
        g_lane = lax.broadcasted_iota(jnp.int32, (feat, lanes), 1)
        for s in range(segs):
            part_s = slice(s * lanes, (s + 1) * lanes)
            G[0, s] = jnp.where(g_lane < rank, g_tok[:, part_s], g_cot[:, part_s]).astype(BF16)
        next(grads)
        for h in range(2):
            g_share(0, h)
        yield

    def fix():
        fix_out = jnp.zeros((rows, feat), F32)
        fix_ig = jnp.zeros((rows, feat), F32)
        for s in range(segs):
            pair = R[s].reshape(feat, lanes)
            mine = Lm[:, s * lanes:(s + 1) * lanes]
            zero = jnp.zeros_like(mine)
            fix_out = fix_out + dot(jnp.where(lane < rank, zero, mine), pair, NT)
            fix_ig = fix_ig + dot(jnp.where(lane < rank, mine, zero), pair, NT)
        acc[0] = acc[0] + fix_out.reshape(2, half_rows, feat)
        Pz[0] = Pz[0] + fix_ig.reshape(2, half_rows, feat)
        yield

    slots = grad.shape[0]
    chunk = min(32, feat)

    def add_grads(i, first):
        off, core = i // CORES, i % CORES
        src = lax.rem(y + off, ny) * CORES + jnp.where(core == 0, c, 1 - c)
        hit = [[(owner[seg[s, src]] == slots * d + q).astype(F32) for s in range(segs)]
               for q in range(slots)]

        def body(r, carry):
            at = pl.ds(pl.multiple_of(r * chunk, chunk), chunk)
            given = [G[i, s, at].astype(F32) for s in range(segs)]
            for q in range(slots):
                value = given[0] * hit[q][0]
                for s in range(1, segs):
                    value = value + given[s] * hit[q][s]
                grad[q, at] = value if first else grad[q, at] + value
            return carry

        lax.fori_loop(0, feat // chunk, body, 0)

    def slots_grad():
        def add(first, count, stride):
            def body(i, carry):
                add_grads(first + i * stride, False)
                return carry

            lax.fori_loop(0, count, body, 0)

        def shared(off):
            for h in range(2):
                arrived(g_piece(off, 1, h), gc_s.at[off, h], gc_r.at[off, h], sibling)

        add_grads(0, True)
        shared(0)
        add(1, 1, 1)
        yield
        if ny > 2:
            add(CORES, 2, CORES * (ny - 2))
            yield
        add(ny, 1, 1)
        for off in range(1, ny):
            if 2 * off != ny:
                shared(off)
        add(CORES + 1, 2 if ny > 2 else 0, CORES * (ny - 2))
        shared(ny // 2)
        add(ny + 1, 1, 1)
        yield

    def partial_ig(off):
        tile = lax.rem(z + off, nz)
        total = jnp.zeros((rows, feat), F32)
        for k in range(nx):
            total = total + dot(C[k].reshape(rows, feat), Wb[k, tile].reshape(feat, feat), NT)
        Pz[off] = total.reshape(2, half_rows, feat)

    def igs():
        def ways(m):
            def body(i, carry):
                partial_ig(m + i * (nz - 2 * m))
                return carry

            lax.fori_loop(0, 2, body, 0)

        partial_ig(nz // 2)
        yield
        for m in range(nz // 2 - 1, 0, -1):
            ways(m)
            yield
        partial_ig(0)
        yield

    def partial_out(m, first):
        tile = lax.rem(z + m, nz)
        block = T[m].reshape(rows, feat)

        def body(k, carry):
            value = dot(block, Wb[k, tile].reshape(feat, feat)).reshape(2, half_rows, feat)
            acc[k] = value if first else acc[k] + value
            return carry

        lax.fori_loop(0, nx, body, 0)

    def outs():
        def ways(m):
            def body(i, carry):
                partial_out(m + i * (nz - 2 * m), False)
                return carry

            lax.fori_loop(0, 2, body, 0)

        partial_out(0, True)
        yield
        for m in range(1, nz // 2):
            ways(m)
            yield
        partial_out(nz // 2, False)
        yield

    own_t.start()
    own_c.start()
    own_a.start()
    own_w.start()

    barrier = pltpu.get_barrier_semaphore()
    partners = (
        [at_mp(m) for m in range(1, nx * nz)]
        + [at_dp(d + m) for m in range(1, nd)]
    )
    for device in partners:
        pl.semaphore_signal(barrier, inc=1, device_id=device, device_id_type=pl.DeviceIdType.MESH)
    pl.semaphore_wait(barrier, len(partners))
    own_t.wait()
    own_c.wait()

    tasks = {
        "W": weights(), "T": gather_t.steps(), "C": gather_c.steps(), "L": lora(), "F": fix(), "G": grads,
        "S": slots_grad(), "i": igs(), "I": scatter_z.steps(ig), "o": outs(), "O": scatter_x.steps(out),
    }
    for name in SCHEDULE:
        next(tasks[name], None)
    for task in tasks.values():
        for _ in task:
            pass

    for copy in pending:
        copy.wait_send()


def local(tokens, base_weight, adapter_pairs, owner_map, seg_adapter, seg_lengths, cotangent):
    rows, feat = tokens.shape
    half = rows // 2
    nz = NZ
    nx = lax.axis_size("mp") // nz
    ny = lax.axis_size("dp") // CORES
    nd = ny * CORES
    stored, depth, lanes = adapter_pairs.shape
    segs = seg_lengths.shape[1]
    total_slots = stored * nx * nz
    slots = total_slots // nd
    piece = feat // nd
    lrows = rows // (nx * nz)
    vmem = lambda shape, dtype: pltpu.VMEM(shape, dtype)
    dma = lambda *shape: pltpu.SemaphoreType.DMA(shape)
    ring = lambda n, pieces=1: [dma(2, 2, pieces, n // 2)] * 2
    pair = lambda *shape: [dma(*shape)] * 2
    scratch = [
        vmem((nz, 2, half, feat), BF16),
        vmem((nx, 2, half, feat), BF16),
        vmem((nx, nz, 2, feat // 2, feat), BF16),
        vmem((total_slots, piece, lanes), BF16),
        vmem((nd, segs, piece, lanes), BF16),
        vmem((segs, nd, piece, lanes), BF16),
        vmem((nx, rows // nx, lanes), F32),
        vmem((nx, rows // nx, lanes), F32),
        vmem((nz, lrows, lanes), F32),
        vmem((nz, lrows, lanes), F32),
        vmem((nx, nz, lrows, lanes), BF16),
        vmem((rows, segs * lanes), BF16),
        vmem((nx, 2, half, feat), F32),
        vmem((nz, 2, half, feat), F32),
        vmem((2, 2, nz // 2, half, feat), BF16),
        vmem((2, 2, nz // 2, half, feat), BF16),
        vmem((2, 2, nx // 2, half, feat), BF16),
        vmem((2, 2, nx // 2, half, feat), BF16),
        vmem((nd, segs, feat, lanes), BF16),
        *ring(nz, QT), *ring(nx), *pair(nx), *ring(ny), *pair(ny, 2),
        *pair(nx * nz), *pair(nd), *pair(nx), *pair(nz), *pair(nz), *pair(nx),
        *ring(nz, QI), *ring(nx), *ring(ny), *pair(ny, 2), dma(4),
    ]
    in_vmem = pl.BlockSpec(memory_space=pltpu.VMEM)
    in_smem = pl.BlockSpec(memory_space=pltpu.SMEM)
    in_any = pl.BlockSpec(memory_space=pl.ANY)
    out, ig, grad = pl.pallas_call(
        functools.partial(kernel, nx, nz, ny),
        out_shape=[
            pltpu.VMEM((2, half, feat), BF16),
            pltpu.VMEM((2, half, feat), BF16),
            pltpu.VMEM((slots, feat, lanes), F32),
        ],
        in_specs=[in_any] * 4 + [in_smem, in_smem, in_smem],
        out_specs=[in_vmem] * 3,
        scratch_shapes=scratch,
        compiler_params=pltpu.CompilerParams(
            collective_id=0, has_side_effects=True, vmem_limit_bytes=56 * 1024 * 1024
        ),
    )(
        tokens.reshape(2, half, feat),
        cotangent.reshape(2, half, feat),
        base_weight.reshape(nx, nz, 2, feat // 2, feat),
        adapter_pairs.reshape(stored, nx, nz, nd, piece, lanes),
        owner_map,
        seg_adapter.T,
        seg_lengths,
    )
    return out.reshape(rows, feat), ig.reshape(rows, feat), grad


def solution(mesh):
    in_specs = (
        P("dp", "mp"),
        P(None, "mp"),
        P("mp", None, None),
        P(),
        P(),
        P("dp", None),
        P("dp", "mp"),
    )
    out_specs = (P("dp", "mp"), P("dp", "mp"), P("dp", "mp", None))
    return jax.shard_map(local, mesh=mesh, in_specs=in_specs, out_specs=out_specs, check_vma=False)
```

```python
import functools

import jax
import jax.numpy as jnp
from jax import lax
from jax.experimental import pallas as pl
from jax.experimental.pallas import tpu as pltpu
from jax.sharding import PartitionSpec as P

NZ = 8
CORES = 2
QT = 1
QI = 1
F32 = jnp.float32
BF16 = jnp.bfloat16
SCHEDULE = "WLTCWCTLTWWTLTWTWCoCiLiIoLTIoLTIioILIoOiOSGIiIOGFSGSOI"
NT = (((1,), (1,)), ((), ()))
TN = (((0,), (0,)), ((), ()))


def dot(a, b, dims=(((1,), (0,)), ((), ()))):
    return lax.dot_general(a, b, dims, preferred_element_type=F32)


def hops(n, way, half):
    return n // 2 if way == half else n // 2 - 1


def kernel(
    nx, nz, ny,
    tok, cot, w, pairs, owner_in, seg_in, lens_in,
    both, grad,
    owner, seg, lens, T, C, Wb, S2, sel, R, Lp, X1, Lz, Z1, Lf, Lm, acc, Pz, zs, zr, xs, xr, G,
    t_s, t_r, c_s, c_r, wx_s, wx_r, wy_s, wy_r, wc_s, wc_r,
    a1_s, a1_r, a3_s, a3_r, lx_s, lx_r, lz_s, lz_r, fz_s, fz_r, fx_s, fx_r,
    rz_s, rz_r, rx_s, rx_r, gy_s, gy_r, gc_s, gc_r, loc,
):
    out = both.at[pl.ds(0, 2)]
    ig = both.at[pl.ds(2, 2)]
    nd = ny * CORES
    d = lax.axis_index("dp")
    j = lax.axis_index("mp")
    y, c = d // CORES, d % CORES
    x, z = j // nz, j % nz
    half_rows, feat = tok.shape[1], tok.shape[2]
    rows = 2 * half_rows
    lanes = 2 * (pairs.shape[-1] // 2)
    rank = lanes // 2
    segs = R.shape[0]
    sibling = (CORES * y + 1 - c, j)

    def at_x(r):
        return (d, lax.rem(r + nx, nx) * nz + z)

    def at_z(r):
        return (d, x * nz + lax.rem(r + nz, nz))

    def at_y(r):
        return (lax.rem(r + ny, ny) * CORES + c, j)

    def at_dp(r):
        return (lax.rem(r + nd, nd), j)

    pending = []

    def remote(src, dst, ssem, rsem, device):
        return pltpu.make_async_remote_copy(
            src_ref=src, dst_ref=dst, send_sem=ssem, recv_sem=rsem,
            device_id=device, device_id_type=pl.DeviceIdType.MESH,
        )

    def send(src, dst, ssem, rsem, device):
        copy = remote(src, dst, ssem, rsem, device)
        copy.start()
        pending.append(copy)

    def arrived(dst, ssem, rsem, device):
        remote(dst, dst, ssem, rsem, device).wait_recv()

    class Fan:
        def __init__(self, count, at, src, dst, landed, ssem, rsem):
            self.count, self.at, self.src, self.dst, self.landed = count, at, src, dst, landed
            self.ssem, self.rsem = ssem, rsem

        def start(self):
            for m in range(1, self.count):
                send(self.src(m), self.dst(m), self.ssem.at[m], self.rsem.at[m], self.at(m))

        def wait(self):
            for m in range(1, self.count):
                arrived(self.landed(m), self.ssem.at[m], self.rsem.at[m], self.at(m))

    class Gather:
        def __init__(self, n, at, me, view, ssem, rsem, absolute=False):
            self.n, self.at, self.me, self.view = n, at, me, view
            self.ssem, self.rsem, self.absolute = ssem, rsem, absolute
            self.pieces = ssem.shape[2]

        def send(self, way, half, piece, step):
            sign = 1 - 2 * way
            src = self.view((-sign * (step - 1)) % self.n, half, piece)
            dst = src if self.absolute else self.view((-sign * step) % self.n, half, piece)
            k = (way, half, piece, step - 1)
            send(src, dst, self.ssem.at[k], self.rsem.at[k], self.at(self.me + sign))

        def start(self):
            for turn in range(2):
                for piece in range(self.pieces):
                    for way in range(2):
                        half = way if turn == 0 else 1 - way
                        if hops(self.n, way, half) >= 1:
                            self.send(way, half, piece, 1)

        def turns(self, step):
            return [turn for turn in range(2) if hops(self.n, 0, turn) >= step]

        def step(self, step, turn, after=None):
            for piece in range(self.pieces):
                for way in range(2):
                    half = way if turn == 0 else 1 - way
                    sign = 1 - 2 * way
                    off = (-sign * step) % self.n
                    k = (way, half, piece, step - 1)
                    arrived(self.view(off, half, piece), self.ssem.at[k], self.rsem.at[k],
                            self.at(self.me + sign))
                    if hops(self.n, way, half) >= step + 1:
                        self.send(way, half, piece, step + 1)
                    if after is not None:
                        after(off, half)

        def steps(self, after=None):
            self.start()
            yield
            for step in range(1, self.n // 2 + 1):
                for turn in self.turns(step):
                    self.step(step, turn, after)
                    yield

    class Scatter:
        def __init__(self, n, at, me, part, sbuf, rbuf, ssem, rsem):
            self.n, self.at, self.me, self.part = n, at, me, part
            self.sbuf, self.rbuf, self.ssem, self.rsem = sbuf, rbuf, ssem, rsem
            self.pieces = ssem.shape[2]
            self.size = part.shape[2] // self.pieces

        def rows(self, piece):
            return pl.ds(piece * self.size, self.size)

        def wait(self, way, half, piece, i):
            k = (way, half, piece, i)
            arrived(self.rbuf.at[way, half, i, self.rows(piece)], self.ssem.at[k],
                    self.rsem.at[k], self.at(self.me + 1 - 2 * way))

        def step(self, i, turn):
            for piece in range(self.pieces):
                for way in range(2):
                    half = way if turn == 0 else 1 - way
                    length = hops(self.n, way, half)
                    sign = 1 - 2 * way
                    k = (way, half, piece, i)
                    at = self.rows(piece)
                    value = self.part[(sign * (length - i)) % self.n, half, at]
                    if i > 0:
                        self.wait(way, half, piece, i - 1)
                        value = value + self.rbuf[way, half, i - 1, at].astype(F32)
                    self.sbuf[way, half, i, at] = value.astype(BF16)
                    send(self.sbuf.at[way, half, i, at], self.rbuf.at[way, half, i, at],
                         self.ssem.at[k], self.rsem.at[k], self.at(self.me + sign))

        def steps(self, result):
            for i in range(self.n // 2):
                for turn in range(2):
                    if i < hops(self.n, 0, turn):
                        self.step(i, turn)
                        yield
            for half in range(2):
                for piece in range(self.pieces):
                    result[half, self.rows(piece)] = self.finish(half, piece)
            yield

        def finish(self, half, piece):
            at = self.rows(piece)
            value = self.part[0, half, at]
            for way in range(2):
                length = hops(self.n, way, half)
                if length >= 1:
                    self.wait(way, half, piece, length - 1)
                    value = value + self.rbuf[way, half, length - 1, at].astype(F32)
            return value.astype(BF16)

    row = lax.broadcasted_iota(jnp.int32, (rows, lanes), 0)
    lane = lax.broadcasted_iota(jnp.int32, (rows, lanes), 1)
    starts = [jnp.int32(0)]

    def mask(s):
        return (row >= starts[s]) & (row < starts[s + 1])

    t_size = half_rows // t_s.shape[2]
    gather_t = Gather(nz, at_z, z, lambda off, h, q: T.at[off, h, pl.ds(q * t_size, t_size)], t_s, t_r)
    gather_c = Gather(nx, at_x, x, lambda off, h, q: C.at[off, h], c_s, c_r)

    def w_piece(off, core, h):
        return Wb.at[pl.ds(1, nx - 1), lax.rem(y + off, ny) * CORES + core, h]

    def g_piece(off, core, h):
        return G.at[CORES * off + core, :, pl.ds(h * (feat // 2), feat // 2)]

    gather_w = Gather(ny, at_y, y, lambda off, h, q: w_piece(off, c, h), wy_s, wy_r, absolute=True)
    gather_g = Gather(ny, at_y, y, lambda off, h, q: g_piece(off, 0, h), gy_s, gy_r)
    scatter_z = Scatter(nz, at_z, z, Pz, zs, zr, rz_s, rz_r)
    scatter_x = Scatter(nx, at_x, x, acc, xs, xr, rx_s, rx_r)

    def w_share(off, h):
        piece = w_piece(off, c, h)
        send(piece, piece, wc_s.at[off, h], wc_r.at[off, h], sibling)

    def g_share(off, h):
        send(g_piece(off, 0, h), g_piece(off, 1, h), gc_s.at[off, h], gc_r.at[off, h], sibling)

    def at_mp(m):
        return (d, lax.rem(x + m // nz, nx) * nz + lax.rem(z + m % nz, nz))

    def from_mp(m):
        return lax.rem(x - m // nz + nx, nx) * nz + lax.rem(z - m % nz + nz, nz)

    fan_a = Fan(
        nx * nz, at_mp,
        lambda m: pairs.at[:, lax.rem(x + m // nz, nx), lax.rem(z + m % nz, nz), d],
        lambda m: S2.at[pl.ds(2 * j, 2)],
        lambda m: S2.at[pl.ds(2 * from_mp(m), 2)], a1_s, a1_r,
    )
    fan_r = Fan(
        nd, lambda m: at_dp(d + m), lambda m: sel.at[m], lambda m: R.at[:, d],
        lambda m: R.at[:, lax.rem(d - m + nd, nd)], a3_s, a3_r,
    )
    fan_lx = Fan(
        nx, lambda k: at_x(x + k), lambda k: Lp.at[lax.rem(x + k, nx)], lambda k: X1.at[k],
        lambda k: X1.at[k], lx_s, lx_r,
    )
    fan_lz = Fan(
        nz, lambda m: at_z(z + m), lambda m: Lz.at[lax.rem(z + m, nz)], lambda m: Z1.at[m],
        lambda m: Z1.at[m], lz_s, lz_r,
    )
    fan_fz = Fan(
        nz, lambda m: at_z(z + m), lambda m: Lf.at[x, z], lambda m: Lf.at[x, z],
        lambda m: Lf.at[x, lax.rem(z - m + nz, nz)], fz_s, fz_r,
    )
    fan_fx = Fan(
        nx, lambda k: at_x(x + k), lambda k: Lf.at[x], lambda k: Lf.at[x],
        lambda k: Lf.at[lax.rem(x - k + nx, nx)], fx_s, fx_r,
    )
    own_s = [
        pltpu.make_async_copy(src, dst, loc.at[4 + i])
        for i, (src, dst) in enumerate(((owner_in, owner), (seg_in, seg), (lens_in, lens)))
    ]
    own_t = pltpu.make_async_copy(tok, T.at[0], loc.at[2])
    own_c = pltpu.make_async_copy(cot, C.at[0], loc.at[3])
    own_w = pltpu.make_async_copy(w.at[x], Wb.at[0], loc.at[0])
    own_a = pltpu.make_async_copy(pairs.at[:, x, z, d], S2.at[pl.ds(2 * j, 2)], loc.at[1])

    def weights():
        for k in range(1, nx):
            send(w.at[lax.rem(x - k + nx, nx), d], Wb.at[k, d], wx_s.at[k], wx_r.at[k], at_x(x - k))
        yield
        for k in range(1, nx):
            arrived(Wb.at[k, d], wx_s.at[k], wx_r.at[k], at_x(x - k))
        steps = gather_w.steps(w_share)
        next(steps)
        for h in range(2):
            w_share(0, h)
        yield
        yield from steps
        own_w.wait()
        for off in range(ny):
            for h in range(2):
                arrived(w_piece(off, 1 - c, h), wc_s.at[off, h], wc_r.at[off, h], sibling)
        yield

    grads = gather_g.steps(g_share)

    def lora():
        fan_a.start()
        yield
        own_a.wait()
        fan_a.wait()
        for m in range(nd):
            other = lax.rem(d + m, nd)
            for s in range(segs):
                sel[m, s] = S2[owner[seg[s, other]]]
        fan_r.start()
        R[:, d] = sel[0]
        yield
        fan_r.wait()
        tok2 = T[0].reshape(rows, feat)
        cot2 = C[0].reshape(rows, feat)
        part = jnp.zeros((rows, lanes), F32)
        for s in range(segs):
            pair = R[s].reshape(feat, lanes)
            both = jnp.where(lane < rank, dot(tok2, pair), dot(cot2, pair))
            part = part + jnp.where(mask(s), both, 0.0)
        Lp[...] = part.reshape(Lp.shape)
        fan_lx.start()
        yield
        fan_lx.wait()
        total = Lp[x]
        for k in range(1, nx):
            total = total + X1[k]
        Lz[...] = total.reshape(Lz.shape).astype(BF16)
        fan_lz.start()
        yield
        fan_lz.wait()
        total = Lz[z].astype(F32)
        for m in range(1, nz):
            total = total + Z1[m].astype(F32)
        Lf[x, z] = pltpu.roll(total, rank, 1).astype(BF16)
        fan_fz.start()
        yield
        fan_fz.wait()
        fan_fx.start()
        yield
        fan_fx.wait()
        both = Lf[...].reshape(rows, lanes)
        for s in range(segs):
            Lm[:, s * lanes:(s + 1) * lanes] = jnp.where(mask(s), both, jnp.zeros_like(both))
        g_tok = dot(T[0].reshape(rows, feat), Lm[...], TN)
        g_cot = dot(C[0].reshape(rows, feat), Lm[...], TN)
        g_lane = lax.broadcasted_iota(jnp.int32, (feat, lanes), 1)
        for s in range(segs):
            part_s = slice(s * lanes, (s + 1) * lanes)
            G[0, s] = jnp.where(g_lane < rank, g_tok[:, part_s], g_cot[:, part_s]).astype(BF16)
        next(grads)
        for h in range(2):
            g_share(0, h)
        yield

    def fix():
        fix_out = jnp.zeros((rows, feat), F32)
        fix_ig = jnp.zeros((rows, feat), F32)
        for s in range(segs):
            pair = R[s].reshape(feat, lanes)
            mine = Lm[:, s * lanes:(s + 1) * lanes]
            zero = jnp.zeros_like(mine)
            fix_out = fix_out + dot(jnp.where(lane < rank, zero, mine), pair, NT)
            fix_ig = fix_ig + dot(jnp.where(lane < rank, mine, zero), pair, NT)
        acc[0] = acc[0] + fix_out.reshape(2, half_rows, feat)
        Pz[0] = Pz[0] + fix_ig.reshape(2, half_rows, feat)
        yield

    slots = grad.shape[0]
    chunk = min(32, feat)

    def add_grads(i, first):
        off, core = i // CORES, i % CORES
        src = lax.rem(y + off, ny) * CORES + jnp.where(core == 0, c, 1 - c)
        hit = [[(owner[seg[s, src]] == slots * d + q).astype(F32) for s in range(segs)]
               for q in range(slots)]

        def body(r, carry):
            at = pl.ds(pl.multiple_of(r * chunk, chunk), chunk)
            given = [G[i, s, at].astype(F32) for s in range(segs)]
            for q in range(slots):
                value = given[0] * hit[q][0]
                for s in range(1, segs):
                    value = value + given[s] * hit[q][s]
                grad[q, at] = value if first else grad[q, at] + value
            return carry

        lax.fori_loop(0, feat // chunk, body, 0)

    def slots_grad():
        def add(first, count, stride):
            def body(i, carry):
                add_grads(first + i * stride, False)
                return carry

            lax.fori_loop(0, count, body, 0)

        def shared(off):
            for h in range(2):
                arrived(g_piece(off, 1, h), gc_s.at[off, h], gc_r.at[off, h], sibling)

        add_grads(0, True)
        shared(0)
        add(1, 1, 1)
        yield
        if ny > 2:
            add(CORES, 2, CORES * (ny - 2))
            yield
        add(ny, 1, 1)
        for off in range(1, ny):
            if 2 * off != ny:
                shared(off)
        add(CORES + 1, 2 if ny > 2 else 0, CORES * (ny - 2))
        shared(ny // 2)
        add(ny + 1, 1, 1)
        yield

    def partial_ig(off):
        tile = lax.rem(z + off, nz)
        total = jnp.zeros((rows, feat), F32)
        for k in range(nx):
            total = total + dot(C[k].reshape(rows, feat), Wb[k, tile].reshape(feat, feat), NT)
        Pz[off] = total.reshape(2, half_rows, feat)

    def igs():
        def ways(m):
            def body(i, carry):
                partial_ig(m + i * (nz - 2 * m))
                return carry

            lax.fori_loop(0, 2, body, 0)

        partial_ig(nz // 2)
        yield
        for m in range(nz // 2 - 1, 0, -1):
            ways(m)
            yield
        partial_ig(0)
        yield

    def partial_out(m, first):
        tile = lax.rem(z + m, nz)
        block = T[m].reshape(rows, feat)

        def body(k, carry):
            value = dot(block, Wb[k, tile].reshape(feat, feat)).reshape(2, half_rows, feat)
            acc[k] = value if first else acc[k] + value
            return carry

        lax.fori_loop(0, nx, body, 0)

    def outs():
        def ways(m):
            def body(i, carry):
                partial_out(m + i * (nz - 2 * m), False)
                return carry

            lax.fori_loop(0, 2, body, 0)

        partial_out(0, True)
        yield
        for m in range(1, nz // 2):
            ways(m)
            yield
        partial_out(nz // 2, False)
        yield

    for copy in own_s:
        copy.start()
    own_t.start()
    own_c.start()
    own_a.start()
    own_w.start()

    barrier = pltpu.get_barrier_semaphore()
    partners = (
        [at_mp(m) for m in range(1, nx * nz)]
        + [at_dp(d + m) for m in range(1, nd)]
    )
    for device in partners:
        pl.semaphore_signal(barrier, inc=1, device_id=device, device_id_type=pl.DeviceIdType.MESH)
    pl.semaphore_wait(barrier, len(partners))
    for copy in own_s:
        copy.wait()
    own_t.wait()
    own_c.wait()
    for s in range(segs):
        starts.append(starts[-1] + lens[0, s])

    tasks = {
        "W": weights(), "T": gather_t.steps(), "C": gather_c.steps(), "L": lora(), "F": fix(), "G": grads,
        "S": slots_grad(), "i": igs(), "I": scatter_z.steps(ig), "o": outs(), "O": scatter_x.steps(out),
    }
    for name in SCHEDULE:
        next(tasks[name], None)
    for task in tasks.values():
        for _ in task:
            pass

    for copy in pending:
        copy.wait_send()


def local(tokens, base_weight, adapter_pairs, owner_map, seg_adapter, seg_lengths, cotangent):
    rows, feat = tokens.shape
    half = rows // 2
    nz = NZ
    nx = lax.axis_size("mp") // nz
    ny = lax.axis_size("dp") // CORES
    nd = ny * CORES
    stored, depth, lanes = adapter_pairs.shape
    segs = seg_lengths.shape[1]
    total_slots = stored * nx * nz
    slots = total_slots // nd
    piece = feat // nd
    lrows = rows // (nx * nz)
    vmem = lambda shape, dtype: pltpu.VMEM(shape, dtype)
    dma = lambda *shape: pltpu.SemaphoreType.DMA(shape)
    ring = lambda n, pieces=1: [dma(2, 2, pieces, n // 2)] * 2
    pair = lambda *shape: [dma(*shape)] * 2
    scratch = [
        pltpu.SMEM(owner_map.shape, jnp.int32),
        pltpu.SMEM((segs, nd), jnp.int32),
        pltpu.SMEM(seg_lengths.shape, jnp.int32),
        vmem((nz, 2, half, feat), BF16),
        vmem((nx, 2, half, feat), BF16),
        vmem((nx, nz, 2, feat // 2, feat), BF16),
        vmem((total_slots, piece, lanes), BF16),
        vmem((nd, segs, piece, lanes), BF16),
        vmem((segs, nd, piece, lanes), BF16),
        vmem((nx, rows // nx, lanes), F32),
        vmem((nx, rows // nx, lanes), F32),
        vmem((nz, lrows, lanes), BF16),
        vmem((nz, lrows, lanes), BF16),
        vmem((nx, nz, lrows, lanes), BF16),
        vmem((rows, segs * lanes), BF16),
        vmem((nx, 2, half, feat), F32),
        vmem((nz, 2, half, feat), F32),
        vmem((2, 2, nz // 2, half, feat), BF16),
        vmem((2, 2, nz // 2, half, feat), BF16),
        vmem((2, 2, nx // 2, half, feat), BF16),
        vmem((2, 2, nx // 2, half, feat), BF16),
        vmem((nd, segs, feat, lanes), BF16),
        *ring(nz, QT), *ring(nx), *pair(nx), *ring(ny), *pair(ny, 2),
        *pair(nx * nz), *pair(nd), *pair(nx), *pair(nz), *pair(nz), *pair(nx),
        *ring(nz, QI), *ring(nx), *ring(ny), *pair(ny, 2), dma(7),
    ]
    in_vmem = pl.BlockSpec(memory_space=pltpu.VMEM)
    in_any = pl.BlockSpec(memory_space=pl.ANY)
    both, grad = pl.pallas_call(
        functools.partial(kernel, nx, nz, ny),
        out_shape=[
            pltpu.VMEM((4, half, feat), BF16),
            pltpu.VMEM((slots, feat, lanes), F32),
        ],
        in_specs=[in_any] * 7,
        out_specs=[in_vmem] * 2,
        scratch_shapes=scratch,
        compiler_params=pltpu.CompilerParams(
            collective_id=0, has_side_effects=True, vmem_limit_bytes=56 * 1024 * 1024
        ),
    )(
        tokens.reshape(2, half, feat),
        cotangent.reshape(2, half, feat),
        base_weight.reshape(nx, nz, 2, feat // 2, feat),
        adapter_pairs.reshape(stored, nx, nz, nd, piece, lanes),
        owner_map,
        seg_adapter.T,
        seg_lengths,
    )
    both = both.reshape(2, rows, feat)
    return both[0], both[1], grad


def solution(mesh):
    in_specs = (
        P("dp", "mp"),
        P(None, "mp"),
        P("mp", None, None),
        P(),
        P(),
        P("dp", None),
        P("dp", "mp"),
    )
    out_specs = (P("dp", "mp"), P("dp", "mp"), P("dp", "mp", None))
    return jax.shard_map(local, mesh=mesh, in_specs=in_specs, out_specs=out_specs, check_vma=False)
```

```python
import functools

import jax
import jax.numpy as jnp
from jax import lax
from jax.experimental import pallas as pl
from jax.experimental.pallas import tpu as pltpu
from jax.sharding import PartitionSpec as P

NZ = 8
CORES = 2
QT = 1
QI = 1
F32 = jnp.float32
BF16 = jnp.bfloat16
SCHEDULE = "WLTCWCTLTWWTLTWTWCoCiLiIoLTIoLTIioILIoOiOSGIiIOGFSGSOI"
NT = (((1,), (1,)), ((), ()))
TN = (((0,), (0,)), ((), ()))


def dot(a, b, dims=(((1,), (0,)), ((), ()))):
    return lax.dot_general(a, b, dims, preferred_element_type=F32)


def hops(n, way, half):
    return n // 2 if way == half else n // 2 - 1


def kernel(
    nx, nz, ny,
    tok, cot, w, pairs, owner_in, seg_in, lens_in,
    both, grad,
    owner, seg, lens, T, C, Wb, S2, sel, R, Lp, X1, Lz, Z1, Lf, Lm, acc, Pz, zs, zr, xs, xr, G,
    t_s, t_r, c_s, c_r, wx_s, wx_r, wy_s, wy_r, wc_s, wc_r,
    a1_s, a1_r, a3_s, a3_r, lx_s, lx_r, lz_s, lz_r, fz_s, fz_r, fx_s, fx_r,
    rz_s, rz_r, rx_s, rx_r, gy_s, gy_r, gc_s, gc_r, loc,
):
    out = both.at[pl.ds(0, 2)]
    ig = both.at[pl.ds(2, 2)]
    nd = ny * CORES
    d = lax.axis_index("dp")
    j = lax.axis_index("mp")
    y, c = d // CORES, d % CORES
    x, z = j // nz, j % nz
    half_rows, feat = tok.shape[1], tok.shape[2]
    rows = 2 * half_rows
    lanes = 2 * (pairs.shape[-1] // 2)
    rank = lanes // 2
    segs = R.shape[0]
    sibling = (CORES * y + 1 - c, j)

    def at_x(r):
        return (d, lax.rem(r + nx, nx) * nz + z)

    def at_z(r):
        return (d, x * nz + lax.rem(r + nz, nz))

    def at_y(r):
        return (lax.rem(r + ny, ny) * CORES + c, j)

    def at_dp(r):
        return (lax.rem(r + nd, nd), j)

    pending = []

    def remote(src, dst, ssem, rsem, device):
        return pltpu.make_async_remote_copy(
            src_ref=src, dst_ref=dst, send_sem=ssem, recv_sem=rsem,
            device_id=device, device_id_type=pl.DeviceIdType.MESH,
        )

    def send(src, dst, ssem, rsem, device):
        copy = remote(src, dst, ssem, rsem, device)
        copy.start()
        pending.append(copy)

    def arrived(dst, ssem, rsem, device):
        remote(dst, dst, ssem, rsem, device).wait_recv()

    class Fan:
        def __init__(self, count, at, src, dst, landed, ssem, rsem):
            self.count, self.at, self.src, self.dst, self.landed = count, at, src, dst, landed
            self.ssem, self.rsem = ssem, rsem

        def start(self):
            def rank_of(m):
                return -min(m % nz, nz - m % nz), m // nz

            for m in sorted(range(1, self.count), key=rank_of):
                send(self.src(m), self.dst(m), self.ssem.at[m], self.rsem.at[m], self.at(m))

        def wait(self):
            for m in range(1, self.count):
                arrived(self.landed(m), self.ssem.at[m], self.rsem.at[m], self.at(m))

    class Gather:
        def __init__(self, n, at, me, view, ssem, rsem, absolute=False):
            self.n, self.at, self.me, self.view = n, at, me, view
            self.ssem, self.rsem, self.absolute = ssem, rsem, absolute
            self.pieces = ssem.shape[2]

        def send(self, way, half, piece, step):
            sign = 1 - 2 * way
            src = self.view((-sign * (step - 1)) % self.n, half, piece)
            dst = src if self.absolute else self.view((-sign * step) % self.n, half, piece)
            k = (way, half, piece, step - 1)
            send(src, dst, self.ssem.at[k], self.rsem.at[k], self.at(self.me + sign))

        def start(self):
            for turn in range(2):
                for piece in range(self.pieces):
                    for way in range(2):
                        half = way if turn == 0 else 1 - way
                        if hops(self.n, way, half) >= 1:
                            self.send(way, half, piece, 1)

        def turns(self, step):
            return [turn for turn in range(2) if hops(self.n, 0, turn) >= step]

        def step(self, step, turn, after=None):
            for piece in range(self.pieces):
                for way in range(2):
                    half = way if turn == 0 else 1 - way
                    sign = 1 - 2 * way
                    off = (-sign * step) % self.n
                    k = (way, half, piece, step - 1)
                    arrived(self.view(off, half, piece), self.ssem.at[k], self.rsem.at[k],
                            self.at(self.me + sign))
                    if hops(self.n, way, half) >= step + 1:
                        self.send(way, half, piece, step + 1)
                    if after is not None:
                        after(off, half)

        def steps(self, after=None):
            self.start()
            yield
            for step in range(1, self.n // 2 + 1):
                for turn in self.turns(step):
                    self.step(step, turn, after)
                    yield

    class Scatter:
        def __init__(self, n, at, me, part, sbuf, rbuf, ssem, rsem):
            self.n, self.at, self.me, self.part = n, at, me, part
            self.sbuf, self.rbuf, self.ssem, self.rsem = sbuf, rbuf, ssem, rsem
            self.pieces = ssem.shape[2]
            self.size = part.shape[2] // self.pieces

        def rows(self, piece):
            return pl.ds(piece * self.size, self.size)

        def wait(self, way, half, piece, i):
            k = (way, half, piece, i)
            arrived(self.rbuf.at[way, half, i, self.rows(piece)], self.ssem.at[k],
                    self.rsem.at[k], self.at(self.me + 1 - 2 * way))

        def step(self, i, turn):
            for piece in range(self.pieces):
                for way in range(2):
                    half = way if turn == 0 else 1 - way
                    length = hops(self.n, way, half)
                    sign = 1 - 2 * way
                    k = (way, half, piece, i)
                    at = self.rows(piece)
                    value = self.part[(sign * (length - i)) % self.n, half, at]
                    if i > 0:
                        self.wait(way, half, piece, i - 1)
                        value = value + self.rbuf[way, half, i - 1, at].astype(F32)
                    self.sbuf[way, half, i, at] = value.astype(BF16)
                    send(self.sbuf.at[way, half, i, at], self.rbuf.at[way, half, i, at],
                         self.ssem.at[k], self.rsem.at[k], self.at(self.me + sign))

        def steps(self, result):
            for i in range(self.n // 2):
                for turn in range(2):
                    if i < hops(self.n, 0, turn):
                        self.step(i, turn)
                        yield
            for half in range(2):
                for piece in range(self.pieces):
                    result[half, self.rows(piece)] = self.finish(half, piece)
            yield

        def finish(self, half, piece):
            at = self.rows(piece)
            value = self.part[0, half, at]
            for way in range(2):
                length = hops(self.n, way, half)
                if length >= 1:
                    self.wait(way, half, piece, length - 1)
                    value = value + self.rbuf[way, half, length - 1, at].astype(F32)
            return value.astype(BF16)

    row = lax.broadcasted_iota(jnp.int32, (rows, lanes), 0)
    lane = lax.broadcasted_iota(jnp.int32, (rows, lanes), 1)
    starts = [jnp.int32(0)]

    def mask(s):
        return (row >= starts[s]) & (row < starts[s + 1])

    t_size = half_rows // t_s.shape[2]
    gather_t = Gather(nz, at_z, z, lambda off, h, q: T.at[off, h, pl.ds(q * t_size, t_size)], t_s, t_r)
    gather_c = Gather(nx, at_x, x, lambda off, h, q: C.at[off, h], c_s, c_r)

    def w_piece(off, core, h):
        return Wb.at[pl.ds(1, nx - 1), lax.rem(y + off, ny) * CORES + core, h]

    def g_piece(off, core, h):
        return G.at[CORES * off + core, :, pl.ds(h * (feat // 2), feat // 2)]

    gather_w = Gather(ny, at_y, y, lambda off, h, q: w_piece(off, c, h), wy_s, wy_r, absolute=True)
    gather_g = Gather(ny, at_y, y, lambda off, h, q: g_piece(off, 0, h), gy_s, gy_r)
    scatter_z = Scatter(nz, at_z, z, Pz, zs, zr, rz_s, rz_r)
    scatter_x = Scatter(nx, at_x, x, acc, xs, xr, rx_s, rx_r)

    def w_share(off, h):
        piece = w_piece(off, c, h)
        send(piece, piece, wc_s.at[off, h], wc_r.at[off, h], sibling)

    def g_share(off, h):
        send(g_piece(off, 0, h), g_piece(off, 1, h), gc_s.at[off, h], gc_r.at[off, h], sibling)

    def at_mp(m):
        return (d, lax.rem(x + m // nz, nx) * nz + lax.rem(z + m % nz, nz))

    def from_mp(m):
        return lax.rem(x - m // nz + nx, nx) * nz + lax.rem(z - m % nz + nz, nz)

    fan_a = Fan(
        nx * nz, at_mp,
        lambda m: pairs.at[:, lax.rem(x + m // nz, nx), lax.rem(z + m % nz, nz), d],
        lambda m: S2.at[pl.ds(2 * j, 2)],
        lambda m: S2.at[pl.ds(2 * from_mp(m), 2)], a1_s, a1_r,
    )
    fan_r = Fan(
        nd, lambda m: at_dp(d + m), lambda m: sel.at[m], lambda m: R.at[:, d],
        lambda m: R.at[:, lax.rem(d - m + nd, nd)], a3_s, a3_r,
    )
    fan_lx = Fan(
        nx, lambda k: at_x(x + k), lambda k: Lp.at[lax.rem(x + k, nx)], lambda k: X1.at[k],
        lambda k: X1.at[k], lx_s, lx_r,
    )
    fan_lz = Fan(
        nz, lambda m: at_z(z + m), lambda m: Lz.at[lax.rem(z + m, nz)], lambda m: Z1.at[m],
        lambda m: Z1.at[m], lz_s, lz_r,
    )
    fan_fz = Fan(
        nz, lambda m: at_z(z + m), lambda m: Lf.at[x, z], lambda m: Lf.at[x, z],
        lambda m: Lf.at[x, lax.rem(z - m + nz, nz)], fz_s, fz_r,
    )
    fan_fx = Fan(
        nx, lambda k: at_x(x + k), lambda k: Lf.at[x], lambda k: Lf.at[x],
        lambda k: Lf.at[lax.rem(x - k + nx, nx)], fx_s, fx_r,
    )
    own_s = [
        pltpu.make_async_copy(src, dst, loc.at[4 + i])
        for i, (src, dst) in enumerate(((owner_in, owner), (seg_in, seg), (lens_in, lens)))
    ]
    own_t = pltpu.make_async_copy(tok, T.at[0], loc.at[2])
    own_c = pltpu.make_async_copy(cot, C.at[0], loc.at[3])
    own_w = pltpu.make_async_copy(w.at[x], Wb.at[0], loc.at[0])
    own_a = pltpu.make_async_copy(pairs.at[:, x, z, d], S2.at[pl.ds(2 * j, 2)], loc.at[1])

    def weights():
        for k in range(1, nx):
            send(w.at[lax.rem(x - k + nx, nx), d], Wb.at[k, d], wx_s.at[k], wx_r.at[k], at_x(x - k))
        yield
        for k in range(1, nx):
            arrived(Wb.at[k, d], wx_s.at[k], wx_r.at[k], at_x(x - k))
        steps = gather_w.steps(w_share)
        next(steps)
        for h in range(2):
            w_share(0, h)
        yield
        yield from steps
        own_w.wait()
        for off in range(ny):
            for h in range(2):
                arrived(w_piece(off, 1 - c, h), wc_s.at[off, h], wc_r.at[off, h], sibling)
        yield

    grads = gather_g.steps(g_share)

    def lora():
        fan_a.start()
        yield
        own_a.wait()
        fan_a.wait()
        for m in range(nd):
            other = lax.rem(d + m, nd)
            for s in range(segs):
                sel[m, s] = S2[owner[seg[s, other]]]
        fan_r.start()
        R[:, d] = sel[0]
        yield
        fan_r.wait()
        tok2 = T[0].reshape(rows, feat)
        cot2 = C[0].reshape(rows, feat)
        part = jnp.zeros((rows, lanes), F32)
        for s in range(segs):
            pair = R[s].reshape(feat, lanes)
            both = jnp.where(lane < rank, dot(tok2, pair), dot(cot2, pair))
            part = part + jnp.where(mask(s), both, 0.0)
        Lp[...] = part.reshape(Lp.shape)
        fan_lx.start()
        yield
        fan_lx.wait()
        total = Lp[x]
        for k in range(1, nx):
            total = total + X1[k]
        Lz[...] = total.reshape(Lz.shape).astype(BF16)
        fan_lz.start()
        yield
        fan_lz.wait()
        total = Lz[z].astype(F32)
        for m in range(1, nz):
            total = total + Z1[m].astype(F32)
        Lf[x, z] = pltpu.roll(total, rank, 1).astype(BF16)
        fan_fz.start()
        yield
        fan_fz.wait()
        fan_fx.start()
        yield
        fan_fx.wait()
        both = Lf[...].reshape(rows, lanes)
        for s in range(segs):
            Lm[:, s * lanes:(s + 1) * lanes] = jnp.where(mask(s), both, jnp.zeros_like(both))
        g_tok = dot(T[0].reshape(rows, feat), Lm[...], TN)
        g_cot = dot(C[0].reshape(rows, feat), Lm[...], TN)
        g_lane = lax.broadcasted_iota(jnp.int32, (feat, lanes), 1)
        for s in range(segs):
            part_s = slice(s * lanes, (s + 1) * lanes)
            G[0, s] = jnp.where(g_lane < rank, g_tok[:, part_s], g_cot[:, part_s]).astype(BF16)
        next(grads)
        for h in range(2):
            g_share(0, h)
        yield

    def fix():
        fix_out = jnp.zeros((rows, feat), F32)
        fix_ig = jnp.zeros((rows, feat), F32)
        for s in range(segs):
            pair = R[s].reshape(feat, lanes)
            mine = Lm[:, s * lanes:(s + 1) * lanes]
            zero = jnp.zeros_like(mine)
            fix_out = fix_out + dot(jnp.where(lane < rank, zero, mine), pair, NT)
            fix_ig = fix_ig + dot(jnp.where(lane < rank, mine, zero), pair, NT)
        acc[0] = acc[0] + fix_out.reshape(2, half_rows, feat)
        Pz[0] = Pz[0] + fix_ig.reshape(2, half_rows, feat)
        yield

    slots = grad.shape[0]
    chunk = min(32, feat)

    def add_grads(i, first):
        off, core = i // CORES, i % CORES
        src = lax.rem(y + off, ny) * CORES + jnp.where(core == 0, c, 1 - c)
        hit = [[(owner[seg[s, src]] == slots * d + q).astype(F32) for s in range(segs)]
               for q in range(slots)]

        def body(r, carry):
            at = pl.ds(pl.multiple_of(r * chunk, chunk), chunk)
            given = [G[i, s, at].astype(F32) for s in range(segs)]
            for q in range(slots):
                value = given[0] * hit[q][0]
                for s in range(1, segs):
                    value = value + given[s] * hit[q][s]
                grad[q, at] = value if first else grad[q, at] + value
            return carry

        lax.fori_loop(0, feat // chunk, body, 0)

    def slots_grad():
        def add(first, count, stride):
            def body(i, carry):
                add_grads(first + i * stride, False)
                return carry

            lax.fori_loop(0, count, body, 0)

        def shared(off):
            for h in range(2):
                arrived(g_piece(off, 1, h), gc_s.at[off, h], gc_r.at[off, h], sibling)

        add_grads(0, True)
        shared(0)
        add(1, 1, 1)
        yield
        if ny > 2:
            add(CORES, 2, CORES * (ny - 2))
            yield
        add(ny, 1, 1)
        for off in range(1, ny):
            if 2 * off != ny:
                shared(off)
        add(CORES + 1, 2 if ny > 2 else 0, CORES * (ny - 2))
        shared(ny // 2)
        add(ny + 1, 1, 1)
        yield

    def partial_ig(off):
        tile = lax.rem(z + off, nz)
        total = jnp.zeros((rows, feat), F32)
        for k in range(nx):
            total = total + dot(C[k].reshape(rows, feat), Wb[k, tile].reshape(feat, feat), NT)
        Pz[off] = total.reshape(2, half_rows, feat)

    def igs():
        def ways(m):
            def body(i, carry):
                partial_ig(m + i * (nz - 2 * m))
                return carry

            lax.fori_loop(0, 2, body, 0)

        partial_ig(nz // 2)
        yield
        for m in range(nz // 2 - 1, 0, -1):
            ways(m)
            yield
        partial_ig(0)
        yield

    def partial_out(m, first):
        tile = lax.rem(z + m, nz)
        block = T[m].reshape(rows, feat)

        def body(k, carry):
            value = dot(block, Wb[k, tile].reshape(feat, feat)).reshape(2, half_rows, feat)
            acc[k] = value if first else acc[k] + value
            return carry

        lax.fori_loop(0, nx, body, 0)

    def outs():
        def ways(m):
            def body(i, carry):
                partial_out(m + i * (nz - 2 * m), False)
                return carry

            lax.fori_loop(0, 2, body, 0)

        partial_out(0, True)
        yield
        for m in range(1, nz // 2):
            ways(m)
            yield
        partial_out(nz // 2, False)
        yield

    for copy in own_s:
        copy.start()
    own_t.start()
    own_c.start()
    own_a.start()
    own_w.start()

    barrier = pltpu.get_barrier_semaphore()
    partners = (
        [at_mp(m) for m in range(1, nx * nz)]
        + [at_dp(d + m) for m in range(1, nd)]
    )
    for device in partners:
        pl.semaphore_signal(barrier, inc=1, device_id=device, device_id_type=pl.DeviceIdType.MESH)
    pl.semaphore_wait(barrier, len(partners))
    for copy in own_s:
        copy.wait()
    own_t.wait()
    own_c.wait()
    for s in range(segs):
        starts.append(starts[-1] + lens[0, s])

    tasks = {
        "W": weights(), "T": gather_t.steps(), "C": gather_c.steps(), "L": lora(), "F": fix(), "G": grads,
        "S": slots_grad(), "i": igs(), "I": scatter_z.steps(ig), "o": outs(), "O": scatter_x.steps(out),
    }
    for name in SCHEDULE:
        next(tasks[name], None)
    for task in tasks.values():
        for _ in task:
            pass

    for copy in pending:
        copy.wait_send()


def local(tokens, base_weight, adapter_pairs, owner_map, seg_adapter, seg_lengths, cotangent):
    rows, feat = tokens.shape
    half = rows // 2
    nz = NZ
    nx = lax.axis_size("mp") // nz
    ny = lax.axis_size("dp") // CORES
    nd = ny * CORES
    stored, depth, lanes = adapter_pairs.shape
    segs = seg_lengths.shape[1]
    total_slots = stored * nx * nz
    slots = total_slots // nd
    piece = feat // nd
    lrows = rows // (nx * nz)
    vmem = lambda shape, dtype: pltpu.VMEM(shape, dtype)
    dma = lambda *shape: pltpu.SemaphoreType.DMA(shape)
    ring = lambda n, pieces=1: [dma(2, 2, pieces, n // 2)] * 2
    pair = lambda *shape: [dma(*shape)] * 2
    scratch = [
        pltpu.SMEM(owner_map.shape, jnp.int32),
        pltpu.SMEM((segs, nd), jnp.int32),
        pltpu.SMEM(seg_lengths.shape, jnp.int32),
        vmem((nz, 2, half, feat), BF16),
        vmem((nx, 2, half, feat), BF16),
        vmem((nx, nz, 2, feat // 2, feat), BF16),
        vmem((total_slots, piece, lanes), BF16),
        vmem((nd, segs, piece, lanes), BF16),
        vmem((segs, nd, piece, lanes), BF16),
        vmem((nx, rows // nx, lanes), F32),
        vmem((nx, rows // nx, lanes), F32),
        vmem((nz, lrows, lanes), BF16),
        vmem((nz, lrows, lanes), BF16),
        vmem((nx, nz, lrows, lanes), BF16),
        vmem((rows, segs * lanes), BF16),
        vmem((nx, 2, half, feat), F32),
        vmem((nz, 2, half, feat), F32),
        vmem((2, 2, nz // 2, half, feat), BF16),
        vmem((2, 2, nz // 2, half, feat), BF16),
        vmem((2, 2, nx // 2, half, feat), BF16),
        vmem((2, 2, nx // 2, half, feat), BF16),
        vmem((nd, segs, feat, lanes), BF16),
        *ring(nz, QT), *ring(nx), *pair(nx), *ring(ny), *pair(ny, 2),
        *pair(nx * nz), *pair(nd), *pair(nx), *pair(nz), *pair(nz), *pair(nx),
        *ring(nz, QI), *ring(nx), *ring(ny), *pair(ny, 2), dma(7),
    ]
    in_vmem = pl.BlockSpec(memory_space=pltpu.VMEM)
    in_any = pl.BlockSpec(memory_space=pl.ANY)
    both, grad = pl.pallas_call(
        functools.partial(kernel, nx, nz, ny),
        out_shape=[
            pltpu.VMEM((4, half, feat), BF16),
            pltpu.VMEM((slots, feat, lanes), F32),
        ],
        in_specs=[in_any] * 7,
        out_specs=[in_vmem] * 2,
        scratch_shapes=scratch,
        compiler_params=pltpu.CompilerParams(
            collective_id=0, has_side_effects=True, vmem_limit_bytes=56 * 1024 * 1024
        ),
    )(
        tokens.reshape(2, half, feat),
        cotangent.reshape(2, half, feat),
        base_weight.reshape(nx, nz, 2, feat // 2, feat),
        adapter_pairs.reshape(stored, nx, nz, nd, piece, lanes),
        owner_map,
        seg_adapter.T,
        seg_lengths,
    )
    both = both.reshape(2, rows, feat)
    return both[0], both[1], grad


def solution(mesh):
    in_specs = (
        P("dp", "mp"),
        P(None, "mp"),
        P("mp", None, None),
        P(),
        P(),
        P("dp", None),
        P("dp", "mp"),
    )
    out_specs = (P("dp", "mp"), P("dp", "mp"), P("dp", "mp", None))
    return jax.shard_map(local, mesh=mesh, in_specs=in_specs, out_specs=out_specs, check_vma=False)
```

```python
import functools

import jax
import jax.numpy as jnp
from jax import lax
from jax.experimental import pallas as pl
from jax.experimental.pallas import tpu as pltpu
from jax.sharding import PartitionSpec as P

NZ = 8
CORES = 2
QT = 1
QI = 1
F32 = jnp.float32
BF16 = jnp.bfloat16
SCHEDULE = "WLTWCTLWTCTLWTWCTWCioLIioTLIioTLIooOILIOSiOiIGFIGSOGSI"
NT = (((1,), (1,)), ((), ()))
TN = (((0,), (0,)), ((), ()))


def dot(a, b, dims=(((1,), (0,)), ((), ()))):
    return lax.dot_general(a, b, dims, preferred_element_type=F32)


def hops(n, way, half):
    return n // 2 if way == half else n // 2 - 1


def kernel(
    nx, nz, ny,
    tok, cot, w, pairs, owner_in, seg_in, lens_in,
    both, grad,
    owner, seg, lens, T, C, Wb, S2, sel, R, Lp, X1, Lz, Z1, Lf, Lm, acc, Pz, zs, zr, xs, xr, G,
    t_s, t_r, c_s, c_r, wx_s, wx_r, wy_s, wy_r, wc_s, wc_r,
    a1_s, a1_r, a3_s, a3_r, lx_s, lx_r, lz_s, lz_r, fz_s, fz_r, fx_s, fx_r,
    rz_s, rz_r, rx_s, rx_r, gy_s, gy_r, gc_s, gc_r, loc,
):
    out = both.at[pl.ds(0, 2)]
    ig = both.at[pl.ds(2, 2)]
    nd = ny * CORES
    d = lax.axis_index("dp")
    j = lax.axis_index("mp")
    y, c = d // CORES, d % CORES
    x, z = j // nz, j % nz
    half_rows, feat = tok.shape[1], tok.shape[2]
    rows = 2 * half_rows
    lanes = 2 * (pairs.shape[-1] // 2)
    rank = lanes // 2
    segs = R.shape[0]
    sibling = (CORES * y + 1 - c, j)

    def at_x(r):
        return (d, lax.rem(r + nx, nx) * nz + z)

    def at_z(r):
        return (d, x * nz + lax.rem(r + nz, nz))

    def at_y(r):
        return (lax.rem(r + ny, ny) * CORES + c, j)

    def at_dp(r):
        return (lax.rem(r + nd, nd), j)

    pending = []

    def remote(src, dst, ssem, rsem, device):
        return pltpu.make_async_remote_copy(
            src_ref=src, dst_ref=dst, send_sem=ssem, recv_sem=rsem,
            device_id=device, device_id_type=pl.DeviceIdType.MESH,
        )

    def send(src, dst, ssem, rsem, device):
        copy = remote(src, dst, ssem, rsem, device)
        copy.start()
        pending.append(copy)

    def arrived(dst, ssem, rsem, device):
        remote(dst, dst, ssem, rsem, device).wait_recv()

    class Fan:
        def __init__(self, count, at, src, dst, landed, ssem, rsem):
            self.count, self.at, self.src, self.dst, self.landed = count, at, src, dst, landed
            self.ssem, self.rsem = ssem, rsem

        def start(self):
            def rank_of(m):
                return -min(m % nz, nz - m % nz), m // nz

            for m in sorted(range(1, self.count), key=rank_of):
                send(self.src(m), self.dst(m), self.ssem.at[m], self.rsem.at[m], self.at(m))

        def wait(self):
            for m in range(1, self.count):
                arrived(self.landed(m), self.ssem.at[m], self.rsem.at[m], self.at(m))

    class Gather:
        def __init__(self, n, at, me, view, ssem, rsem, absolute=False):
            self.n, self.at, self.me, self.view = n, at, me, view
            self.ssem, self.rsem, self.absolute = ssem, rsem, absolute
            self.pieces = ssem.shape[2]

        def send(self, way, half, piece, step):
            sign = 1 - 2 * way
            src = self.view((-sign * (step - 1)) % self.n, half, piece)
            dst = src if self.absolute else self.view((-sign * step) % self.n, half, piece)
            k = (way, half, piece, step - 1)
            send(src, dst, self.ssem.at[k], self.rsem.at[k], self.at(self.me + sign))

        def start(self):
            for turn in range(2):
                for piece in range(self.pieces):
                    for way in range(2):
                        half = way if turn == 0 else 1 - way
                        if hops(self.n, way, half) >= 1:
                            self.send(way, half, piece, 1)

        def turns(self, step):
            return [turn for turn in range(2) if hops(self.n, 0, turn) >= step]

        def step(self, step, turn, after=None):
            for piece in range(self.pieces):
                for way in range(2):
                    half = way if turn == 0 else 1 - way
                    sign = 1 - 2 * way
                    off = (-sign * step) % self.n
                    k = (way, half, piece, step - 1)
                    arrived(self.view(off, half, piece), self.ssem.at[k], self.rsem.at[k],
                            self.at(self.me + sign))
                    if hops(self.n, way, half) >= step + 1:
                        self.send(way, half, piece, step + 1)
                    if after is not None:
                        after(off, half)

        def steps(self, after=None):
            self.start()
            yield
            for step in range(1, self.n // 2 + 1):
                for turn in self.turns(step):
                    self.step(step, turn, after)
                    yield

    class Scatter:
        def __init__(self, n, at, me, part, sbuf, rbuf, ssem, rsem):
            self.n, self.at, self.me, self.part = n, at, me, part
            self.sbuf, self.rbuf, self.ssem, self.rsem = sbuf, rbuf, ssem, rsem
            self.pieces = ssem.shape[2]
            self.size = part.shape[2] // self.pieces

        def rows(self, piece):
            return pl.ds(piece * self.size, self.size)

        def wait(self, way, half, piece, i):
            k = (way, half, piece, i)
            arrived(self.rbuf.at[way, half, i, self.rows(piece)], self.ssem.at[k],
                    self.rsem.at[k], self.at(self.me + 1 - 2 * way))

        def step(self, i, turn):
            for piece in range(self.pieces):
                for way in range(2):
                    half = way if turn == 0 else 1 - way
                    length = hops(self.n, way, half)
                    sign = 1 - 2 * way
                    k = (way, half, piece, i)
                    at = self.rows(piece)
                    value = self.part[(sign * (length - i)) % self.n, half, at]
                    if i > 0:
                        self.wait(way, half, piece, i - 1)
                        value = value + self.rbuf[way, half, i - 1, at].astype(F32)
                    self.sbuf[way, half, i, at] = value.astype(BF16)
                    send(self.sbuf.at[way, half, i, at], self.rbuf.at[way, half, i, at],
                         self.ssem.at[k], self.rsem.at[k], self.at(self.me + sign))

        def steps(self, result):
            for i in range(self.n // 2):
                for turn in range(2):
                    if i < hops(self.n, 0, turn):
                        self.step(i, turn)
                        yield
            for half in range(2):
                for piece in range(self.pieces):
                    result[half, self.rows(piece)] = self.finish(half, piece)
            yield

        def finish(self, half, piece):
            at = self.rows(piece)
            value = self.part[0, half, at]
            for way in range(2):
                length = hops(self.n, way, half)
                if length >= 1:
                    self.wait(way, half, piece, length - 1)
                    value = value + self.rbuf[way, half, length - 1, at].astype(F32)
            return value.astype(BF16)

    row = lax.broadcasted_iota(jnp.int32, (rows, lanes), 0)
    lane = lax.broadcasted_iota(jnp.int32, (rows, lanes), 1)
    starts = [jnp.int32(0)]

    def mask(s):
        return (row >= starts[s]) & (row < starts[s + 1])

    t_size = half_rows // t_s.shape[2]
    gather_t = Gather(nz, at_z, z, lambda off, h, q: T.at[off, h, pl.ds(q * t_size, t_size)], t_s, t_r)
    gather_c = Gather(nx, at_x, x, lambda off, h, q: C.at[off, h], c_s, c_r)

    def w_piece(off, core, h):
        return Wb.at[pl.ds(1, nx - 1), lax.rem(y + off, ny) * CORES + core, h]

    def g_piece(off, core, h):
        return G.at[CORES * off + core, :, pl.ds(h * (feat // 2), feat // 2)]

    gather_w = Gather(ny, at_y, y, lambda off, h, q: w_piece(off, c, h), wy_s, wy_r, absolute=True)
    gather_g = Gather(ny, at_y, y, lambda off, h, q: g_piece(off, 0, h), gy_s, gy_r)
    scatter_z = Scatter(nz, at_z, z, Pz, zs, zr, rz_s, rz_r)
    scatter_x = Scatter(nx, at_x, x, acc, xs, xr, rx_s, rx_r)

    def w_share(off, h):
        piece = w_piece(off, c, h)
        send(piece, piece, wc_s.at[off, h], wc_r.at[off, h], sibling)

    def g_share(off, h):
        send(g_piece(off, 0, h), g_piece(off, 1, h), gc_s.at[off, h], gc_r.at[off, h], sibling)

    def at_mp(m):
        return (d, lax.rem(x + m // nz, nx) * nz + lax.rem(z + m % nz, nz))

    def from_mp(m):
        return lax.rem(x - m // nz + nx, nx) * nz + lax.rem(z - m % nz + nz, nz)

    fan_a = Fan(
        nx * nz, at_mp,
        lambda m: pairs.at[:, lax.rem(x + m // nz, nx), lax.rem(z + m % nz, nz), d],
        lambda m: S2.at[pl.ds(2 * j, 2)],
        lambda m: S2.at[pl.ds(2 * from_mp(m), 2)], a1_s, a1_r,
    )
    fan_r = Fan(
        nd, lambda m: at_dp(d + m), lambda m: sel.at[m], lambda m: R.at[:, d],
        lambda m: R.at[:, lax.rem(d - m + nd, nd)], a3_s, a3_r,
    )
    fan_lx = Fan(
        nx, lambda k: at_x(x + k), lambda k: Lp.at[lax.rem(x + k, nx)], lambda k: X1.at[k],
        lambda k: X1.at[k], lx_s, lx_r,
    )
    fan_lz = Fan(
        nz, lambda m: at_z(z + m), lambda m: Lz.at[lax.rem(z + m, nz)], lambda m: Z1.at[m],
        lambda m: Z1.at[m], lz_s, lz_r,
    )
    fan_fz = Fan(
        nz, lambda m: at_z(z + m), lambda m: Lf.at[x, z], lambda m: Lf.at[x, z],
        lambda m: Lf.at[x, lax.rem(z - m + nz, nz)], fz_s, fz_r,
    )
    fan_fx = Fan(
        nx, lambda k: at_x(x + k), lambda k: Lf.at[x], lambda k: Lf.at[x],
        lambda k: Lf.at[lax.rem(x - k + nx, nx)], fx_s, fx_r,
    )
    own_s = [
        pltpu.make_async_copy(src, dst, loc.at[4 + i])
        for i, (src, dst) in enumerate(((owner_in, owner), (seg_in, seg), (lens_in, lens)))
    ]
    own_t = pltpu.make_async_copy(tok, T.at[0], loc.at[2])
    own_c = pltpu.make_async_copy(cot, C.at[0], loc.at[3])
    own_w = pltpu.make_async_copy(w.at[x], Wb.at[0], loc.at[0])
    own_a = pltpu.make_async_copy(pairs.at[:, x, z, d], S2.at[pl.ds(2 * j, 2)], loc.at[1])

    def weights():
        for k in range(1, nx):
            send(w.at[lax.rem(x - k + nx, nx), d], Wb.at[k, d], wx_s.at[k], wx_r.at[k], at_x(x - k))
        yield
        for k in range(1, nx):
            arrived(Wb.at[k, d], wx_s.at[k], wx_r.at[k], at_x(x - k))
        steps = gather_w.steps(w_share)
        next(steps)
        for h in range(2):
            w_share(0, h)
        yield
        yield from steps
        own_w.wait()
        for off in range(ny):
            for h in range(2):
                arrived(w_piece(off, 1 - c, h), wc_s.at[off, h], wc_r.at[off, h], sibling)
        yield

    grads = gather_g.steps(g_share)

    def lora():
        fan_a.start()
        yield
        own_a.wait()
        fan_a.wait()
        for m in range(nd):
            other = lax.rem(d + m, nd)
            for s in range(segs):
                sel[m, s] = S2[owner[seg[s, other]]]
        fan_r.start()
        R[:, d] = sel[0]
        yield
        fan_r.wait()
        tok2 = T[0].reshape(rows, feat)
        cot2 = C[0].reshape(rows, feat)
        part = jnp.zeros((rows, lanes), F32)
        for s in range(segs):
            pair = R[s].reshape(feat, lanes)
            both = jnp.where(lane < rank, dot(tok2, pair), dot(cot2, pair))
            part = part + jnp.where(mask(s), both, 0.0)
        Lp[...] = part.reshape(Lp.shape)
        fan_lx.start()
        yield
        fan_lx.wait()
        total = Lp[x]
        for k in range(1, nx):
            total = total + X1[k]
        Lz[...] = total.reshape(Lz.shape).astype(BF16)
        fan_lz.start()
        yield
        fan_lz.wait()
        total = Lz[z].astype(F32)
        for m in range(1, nz):
            total = total + Z1[m].astype(F32)
        Lf[x, z] = pltpu.roll(total, rank, 1).astype(BF16)
        fan_fz.start()
        yield
        fan_fz.wait()
        fan_fx.start()
        yield
        fan_fx.wait()
        both = Lf[...].reshape(rows, lanes)
        for s in range(segs):
            Lm[:, s * lanes:(s + 1) * lanes] = jnp.where(mask(s), both, jnp.zeros_like(both))
        g_tok = dot(T[0].reshape(rows, feat), Lm[...], TN)
        g_cot = dot(C[0].reshape(rows, feat), Lm[...], TN)
        g_lane = lax.broadcasted_iota(jnp.int32, (feat, lanes), 1)
        for s in range(segs):
            part_s = slice(s * lanes, (s + 1) * lanes)
            G[0, s] = jnp.where(g_lane < rank, g_tok[:, part_s], g_cot[:, part_s]).astype(BF16)
        next(grads)
        for h in range(2):
            g_share(0, h)
        yield

    def fix():
        fix_out = jnp.zeros((rows, feat), F32)
        fix_ig = jnp.zeros((rows, feat), F32)
        for s in range(segs):
            pair = R[s].reshape(feat, lanes)
            mine = Lm[:, s * lanes:(s + 1) * lanes]
            zero = jnp.zeros_like(mine)
            fix_out = fix_out + dot(jnp.where(lane < rank, zero, mine), pair, NT)
            fix_ig = fix_ig + dot(jnp.where(lane < rank, mine, zero), pair, NT)
        acc[0] = acc[0] + fix_out.reshape(2, half_rows, feat)
        Pz[0] = Pz[0] + fix_ig.reshape(2, half_rows, feat)
        yield

    slots = grad.shape[0]
    chunk = min(32, feat)

    def add_grads(i, first):
        off, core = i // CORES, i % CORES
        src = lax.rem(y + off, ny) * CORES + jnp.where(core == 0, c, 1 - c)
        hit = [[(owner[seg[s, src]] == slots * d + q).astype(F32) for s in range(segs)]
               for q in range(slots)]

        def body(r, carry):
            at = pl.ds(pl.multiple_of(r * chunk, chunk), chunk)
            given = [G[i, s, at].astype(F32) for s in range(segs)]
            for q in range(slots):
                value = given[0] * hit[q][0]
                for s in range(1, segs):
                    value = value + given[s] * hit[q][s]
                grad[q, at] = value if first else grad[q, at] + value
            return carry

        lax.fori_loop(0, feat // chunk, body, 0)

    def slots_grad():
        def add(first, count, stride):
            def body(i, carry):
                add_grads(first + i * stride, False)
                return carry

            lax.fori_loop(0, count, body, 0)

        def shared(off):
            for h in range(2):
                arrived(g_piece(off, 1, h), gc_s.at[off, h], gc_r.at[off, h], sibling)

        add_grads(0, True)
        shared(0)
        add(1, 1, 1)
        yield
        if ny > 2:
            add(CORES, 2, CORES * (ny - 2))
            yield
        add(ny, 1, 1)
        for off in range(1, ny):
            if 2 * off != ny:
                shared(off)
        add(CORES + 1, 2 if ny > 2 else 0, CORES * (ny - 2))
        shared(ny // 2)
        add(ny + 1, 1, 1)
        yield

    def partial_ig(off):
        tile = lax.rem(z + off, nz)
        total = jnp.zeros((rows, feat), F32)
        for k in range(nx):
            total = total + dot(C[k].reshape(rows, feat), Wb[k, tile].reshape(feat, feat), NT)
        Pz[off] = total.reshape(2, half_rows, feat)

    def igs():
        def ways(m):
            def body(i, carry):
                partial_ig(m + i * (nz - 2 * m))
                return carry

            lax.fori_loop(0, 2, body, 0)

        partial_ig(nz // 2)
        yield
        for m in range(nz // 2 - 1, 0, -1):
            ways(m)
            yield
        partial_ig(0)
        yield

    def partial_out(m, first):
        tile = lax.rem(z + m, nz)
        block = T[m].reshape(rows, feat)

        def body(k, carry):
            value = dot(block, Wb[k, tile].reshape(feat, feat)).reshape(2, half_rows, feat)
            acc[k] = value if first else acc[k] + value
            return carry

        lax.fori_loop(0, nx, body, 0)

    def outs():
        def ways(m):
            def body(i, carry):
                partial_out(m + i * (nz - 2 * m), False)
                return carry

            lax.fori_loop(0, 2, body, 0)

        partial_out(0, True)
        yield
        for m in range(1, nz // 2):
            ways(m)
            yield
        partial_out(nz // 2, False)
        yield

    for copy in own_s:
        copy.start()
    own_t.start()
    own_c.start()
    own_a.start()
    own_w.start()

    barrier = pltpu.get_barrier_semaphore()
    partners = (
        [at_mp(m) for m in range(1, nx * nz)]
        + [at_dp(d + m) for m in range(1, nd)]
    )
    for device in partners:
        pl.semaphore_signal(barrier, inc=1, device_id=device, device_id_type=pl.DeviceIdType.MESH)
    pl.semaphore_wait(barrier, len(partners))
    for copy in own_s:
        copy.wait()
    own_t.wait()
    own_c.wait()
    for s in range(segs):
        starts.append(starts[-1] + lens[0, s])

    tasks = {
        "W": weights(), "T": gather_t.steps(), "C": gather_c.steps(), "L": lora(), "F": fix(), "G": grads,
        "S": slots_grad(), "i": igs(), "I": scatter_z.steps(ig), "o": outs(), "O": scatter_x.steps(out),
    }
    for name in SCHEDULE:
        next(tasks[name], None)
    for task in tasks.values():
        for _ in task:
            pass

    for copy in pending:
        copy.wait_send()


def local(tokens, base_weight, adapter_pairs, owner_map, seg_adapter, seg_lengths, cotangent):
    rows, feat = tokens.shape
    half = rows // 2
    nz = NZ
    nx = lax.axis_size("mp") // nz
    ny = lax.axis_size("dp") // CORES
    nd = ny * CORES
    stored, depth, lanes = adapter_pairs.shape
    segs = seg_lengths.shape[1]
    total_slots = stored * nx * nz
    slots = total_slots // nd
    piece = feat // nd
    lrows = rows // (nx * nz)
    vmem = lambda shape, dtype: pltpu.VMEM(shape, dtype)
    dma = lambda *shape: pltpu.SemaphoreType.DMA(shape)
    ring = lambda n, pieces=1: [dma(2, 2, pieces, n // 2)] * 2
    pair = lambda *shape: [dma(*shape)] * 2
    scratch = [
        pltpu.SMEM(owner_map.shape, jnp.int32),
        pltpu.SMEM((segs, nd), jnp.int32),
        pltpu.SMEM(seg_lengths.shape, jnp.int32),
        vmem((nz, 2, half, feat), BF16),
        vmem((nx, 2, half, feat), BF16),
        vmem((nx, nz, 2, feat // 2, feat), BF16),
        vmem((total_slots, piece, lanes), BF16),
        vmem((nd, segs, piece, lanes), BF16),
        vmem((segs, nd, piece, lanes), BF16),
        vmem((nx, rows // nx, lanes), F32),
        vmem((nx, rows // nx, lanes), F32),
        vmem((nz, lrows, lanes), BF16),
        vmem((nz, lrows, lanes), BF16),
        vmem((nx, nz, lrows, lanes), BF16),
        vmem((rows, segs * lanes), BF16),
        vmem((nx, 2, half, feat), F32),
        vmem((nz, 2, half, feat), F32),
        vmem((2, 2, nz // 2, half, feat), BF16),
        vmem((2, 2, nz // 2, half, feat), BF16),
        vmem((2, 2, nx // 2, half, feat), BF16),
        vmem((2, 2, nx // 2, half, feat), BF16),
        vmem((nd, segs, feat, lanes), BF16),
        *ring(nz, QT), *ring(nx), *pair(nx), *ring(ny), *pair(ny, 2),
        *pair(nx * nz), *pair(nd), *pair(nx), *pair(nz), *pair(nz), *pair(nx),
        *ring(nz, QI), *ring(nx), *ring(ny), *pair(ny, 2), dma(7),
    ]
    in_vmem = pl.BlockSpec(memory_space=pltpu.VMEM)
    in_any = pl.BlockSpec(memory_space=pl.ANY)
    both, grad = pl.pallas_call(
        functools.partial(kernel, nx, nz, ny),
        out_shape=[
            pltpu.VMEM((4, half, feat), BF16),
            pltpu.VMEM((slots, feat, lanes), F32),
        ],
        in_specs=[in_any] * 7,
        out_specs=[in_vmem] * 2,
        scratch_shapes=scratch,
        compiler_params=pltpu.CompilerParams(
            collective_id=0, has_side_effects=True, vmem_limit_bytes=56 * 1024 * 1024
        ),
    )(
        tokens.reshape(2, half, feat),
        cotangent.reshape(2, half, feat),
        base_weight.reshape(nx, nz, 2, feat // 2, feat),
        adapter_pairs.reshape(stored, nx, nz, nd, piece, lanes),
        owner_map,
        seg_adapter.T,
        seg_lengths,
    )
    both = both.reshape(2, rows, feat)
    return both[0], both[1], grad


def solution(mesh):
    in_specs = (
        P("dp", "mp"),
        P(None, "mp"),
        P("mp", None, None),
        P(),
        P(),
        P("dp", None),
        P("dp", "mp"),
    )
    out_specs = (P("dp", "mp"), P("dp", "mp"), P("dp", "mp", None))
    return jax.shard_map(local, mesh=mesh, in_specs=in_specs, out_specs=out_specs, check_vma=False)
```

```python
import functools

import jax
import jax.numpy as jnp
from jax import lax
from jax.experimental import pallas as pl
from jax.experimental.pallas import tpu as pltpu
from jax.sharding import PartitionSpec as P

NZ = 8
CORES = 2
QT = 1
QI = 1
F32 = jnp.float32
BF16 = jnp.bfloat16
SCHEDULE = "WLTWCTLWTCTLWTWCTWCioLIioTLIioTLIooOILIOSiOiIGFIGSOGSI"
NT = (((1,), (1,)), ((), ()))
TN = (((0,), (0,)), ((), ()))


def dot(a, b, dims=(((1,), (0,)), ((), ()))):
    return lax.dot_general(a, b, dims, preferred_element_type=F32)


def hops(n, way, half):
    return n // 2 if way == half else n // 2 - 1


def kernel(
    nx, nz, ny,
    tok, cot, w, pairs, owner_in, seg_in, lens_in,
    both, grad,
    owner, seg, lens, T, C, Wb, S2, sel, R, Lp, X1, Lz, Z1, Lf, Lm, acc, Pz, zs, zr, xs, xr, G,
    t_s, t_r, c_s, c_r, wx_s, wx_r, wy_s, wy_r, wc_s, wc_r,
    a1_s, a1_r, a3_s, a3_r, lx_s, lx_r, lz_s, lz_r, fz_s, fz_r, fx_s, fx_r,
    rz_s, rz_r, rx_s, rx_r, gy_s, gy_r, gc_s, gc_r, loc,
):
    out = both.at[pl.ds(0, 2)]
    ig = both.at[pl.ds(2, 2)]
    nd = ny * CORES
    d = lax.axis_index("dp")
    j = lax.axis_index("mp")
    y, c = d // CORES, d % CORES
    x, z = j // nz, j % nz
    half_rows, feat = tok.shape[1], tok.shape[2]
    rows = 2 * half_rows
    lanes = 2 * (pairs.shape[-1] // 2)
    rank = lanes // 2
    segs = R.shape[0]
    sibling = (CORES * y + 1 - c, j)

    def at_x(r):
        return (d, lax.rem(r + nx, nx) * nz + z)

    def at_z(r):
        return (d, x * nz + lax.rem(r + nz, nz))

    def at_y(r):
        return (lax.rem(r + ny, ny) * CORES + c, j)

    def at_dp(r):
        return (lax.rem(r + nd, nd), j)

    pending = []

    def remote(src, dst, ssem, rsem, device):
        return pltpu.make_async_remote_copy(
            src_ref=src, dst_ref=dst, send_sem=ssem, recv_sem=rsem,
            device_id=device, device_id_type=pl.DeviceIdType.MESH,
        )

    def send(src, dst, ssem, rsem, device):
        copy = remote(src, dst, ssem, rsem, device)
        copy.start()
        pending.append(copy)

    def arrived(dst, ssem, rsem, device):
        remote(dst, dst, ssem, rsem, device).wait_recv()

    class Fan:
        def __init__(self, count, at, src, dst, landed, ssem, rsem):
            self.count, self.at, self.src, self.dst, self.landed = count, at, src, dst, landed
            self.ssem, self.rsem = ssem, rsem

        def start(self):
            def rank_of(m):
                return -min(m % nz, nz - m % nz), m // nz

            for m in sorted(range(1, self.count), key=rank_of):
                self.send(m)

        def send(self, m):
            send(self.src(m), self.dst(m), self.ssem.at[m], self.rsem.at[m], self.at(m))

        def wait(self):
            for m in range(1, self.count):
                arrived(self.landed(m), self.ssem.at[m], self.rsem.at[m], self.at(m))

    class Gather:
        def __init__(self, n, at, me, view, ssem, rsem, absolute=False):
            self.n, self.at, self.me, self.view = n, at, me, view
            self.ssem, self.rsem, self.absolute = ssem, rsem, absolute
            self.pieces = ssem.shape[2]

        def send(self, way, half, piece, step):
            sign = 1 - 2 * way
            src = self.view((-sign * (step - 1)) % self.n, half, piece)
            dst = src if self.absolute else self.view((-sign * step) % self.n, half, piece)
            k = (way, half, piece, step - 1)
            send(src, dst, self.ssem.at[k], self.rsem.at[k], self.at(self.me + sign))

        def start(self):
            for turn in range(2):
                for piece in range(self.pieces):
                    for way in range(2):
                        half = way if turn == 0 else 1 - way
                        if hops(self.n, way, half) >= 1:
                            self.send(way, half, piece, 1)

        def turns(self, step):
            return [turn for turn in range(2) if hops(self.n, 0, turn) >= step]

        def step(self, step, turn, after=None):
            for piece in range(self.pieces):
                for way in range(2):
                    half = way if turn == 0 else 1 - way
                    sign = 1 - 2 * way
                    off = (-sign * step) % self.n
                    k = (way, half, piece, step - 1)
                    arrived(self.view(off, half, piece), self.ssem.at[k], self.rsem.at[k],
                            self.at(self.me + sign))
                    if hops(self.n, way, half) >= step + 1:
                        self.send(way, half, piece, step + 1)
                    if after is not None:
                        after(off, half)

        def steps(self, after=None):
            self.start()
            yield
            for step in range(1, self.n // 2 + 1):
                for turn in self.turns(step):
                    self.step(step, turn, after)
                    yield

    class Scatter:
        def __init__(self, n, at, me, part, sbuf, rbuf, ssem, rsem):
            self.n, self.at, self.me, self.part = n, at, me, part
            self.sbuf, self.rbuf, self.ssem, self.rsem = sbuf, rbuf, ssem, rsem
            self.pieces = ssem.shape[2]
            self.size = part.shape[2] // self.pieces

        def rows(self, piece):
            return pl.ds(piece * self.size, self.size)

        def wait(self, way, half, piece, i):
            k = (way, half, piece, i)
            arrived(self.rbuf.at[way, half, i, self.rows(piece)], self.ssem.at[k],
                    self.rsem.at[k], self.at(self.me + 1 - 2 * way))

        def step(self, i, turn):
            for piece in range(self.pieces):
                for way in range(2):
                    half = way if turn == 0 else 1 - way
                    length = hops(self.n, way, half)
                    sign = 1 - 2 * way
                    k = (way, half, piece, i)
                    at = self.rows(piece)
                    value = self.part[(sign * (length - i)) % self.n, half, at]
                    if i > 0:
                        self.wait(way, half, piece, i - 1)
                        value = value + self.rbuf[way, half, i - 1, at].astype(F32)
                    self.sbuf[way, half, i, at] = value.astype(BF16)
                    send(self.sbuf.at[way, half, i, at], self.rbuf.at[way, half, i, at],
                         self.ssem.at[k], self.rsem.at[k], self.at(self.me + sign))

        def steps(self, result):
            for i in range(self.n // 2):
                for turn in range(2):
                    if i < hops(self.n, 0, turn):
                        self.step(i, turn)
                        yield
            for half in range(2):
                for piece in range(self.pieces):
                    result[half, self.rows(piece)] = self.finish(half, piece)
            yield

        def finish(self, half, piece):
            at = self.rows(piece)
            value = self.part[0, half, at]
            for way in range(2):
                length = hops(self.n, way, half)
                if length >= 1:
                    self.wait(way, half, piece, length - 1)
                    value = value + self.rbuf[way, half, length - 1, at].astype(F32)
            return value.astype(BF16)

    row = lax.broadcasted_iota(jnp.int32, (rows, lanes), 0)
    lane = lax.broadcasted_iota(jnp.int32, (rows, lanes), 1)
    starts = [jnp.int32(0)]

    def mask(s):
        return (row >= starts[s]) & (row < starts[s + 1])

    t_size = half_rows // t_s.shape[2]
    gather_t = Gather(nz, at_z, z, lambda off, h, q: T.at[off, h, pl.ds(q * t_size, t_size)], t_s, t_r)
    gather_c = Gather(nx, at_x, x, lambda off, h, q: C.at[off, h], c_s, c_r)

    def w_piece(off, core, h):
        return Wb.at[pl.ds(1, nx - 1), lax.rem(y + off, ny) * CORES + core, h]

    def g_piece(off, core, h):
        return G.at[CORES * off + core, :, pl.ds(h * (feat // 2), feat // 2)]

    gather_w = Gather(ny, at_y, y, lambda off, h, q: w_piece(off, c, h), wy_s, wy_r, absolute=True)
    gather_g = Gather(ny, at_y, y, lambda off, h, q: g_piece(off, 0, h), gy_s, gy_r)
    scatter_z = Scatter(nz, at_z, z, Pz, zs, zr, rz_s, rz_r)
    scatter_x = Scatter(nx, at_x, x, acc, xs, xr, rx_s, rx_r)

    def w_share(off, h):
        piece = w_piece(off, c, h)
        send(piece, piece, wc_s.at[off, h], wc_r.at[off, h], sibling)

    def g_share(off, h):
        send(g_piece(off, 0, h), g_piece(off, 1, h), gc_s.at[off, h], gc_r.at[off, h], sibling)

    def at_mp(m):
        return (d, lax.rem(x + m // nz, nx) * nz + lax.rem(z + m % nz, nz))

    def from_mp(m):
        return lax.rem(x - m // nz + nx, nx) * nz + lax.rem(z - m % nz + nz, nz)

    fan_a = Fan(
        nx * nz, at_mp,
        lambda m: pairs.at[:, lax.rem(x + m // nz, nx), lax.rem(z + m % nz, nz), d],
        lambda m: S2.at[pl.ds(2 * j, 2)],
        lambda m: S2.at[pl.ds(2 * from_mp(m), 2)], a1_s, a1_r,
    )
    fan_r = Fan(
        nd, lambda m: at_dp(d + m), lambda m: sel.at[m], lambda m: R.at[:, d],
        lambda m: R.at[:, lax.rem(d - m + nd, nd)], a3_s, a3_r,
    )
    fan_lx = Fan(
        nx, lambda k: at_x(x + k), lambda k: Lp.at[lax.rem(x + k, nx)], lambda k: X1.at[k],
        lambda k: X1.at[k], lx_s, lx_r,
    )
    fan_lz = Fan(
        nz, lambda m: at_z(z + m), lambda m: Lz.at[lax.rem(z + m, nz)], lambda m: Z1.at[m],
        lambda m: Z1.at[m], lz_s, lz_r,
    )
    fan_fz = Fan(
        nz, lambda m: at_z(z + m), lambda m: Lf.at[x, z], lambda m: Lf.at[x, z],
        lambda m: Lf.at[x, lax.rem(z - m + nz, nz)], fz_s, fz_r,
    )
    fan_fx = Fan(
        nx, lambda k: at_x(x + k), lambda k: Lf.at[x], lambda k: Lf.at[x],
        lambda k: Lf.at[lax.rem(x - k + nx, nx)], fx_s, fx_r,
    )
    own_s = [
        pltpu.make_async_copy(src, dst, loc.at[4 + i])
        for i, (src, dst) in enumerate(((owner_in, owner), (seg_in, seg), (lens_in, lens)))
    ]
    own_t = pltpu.make_async_copy(tok, T.at[0], loc.at[2])
    own_c = pltpu.make_async_copy(cot, C.at[0], loc.at[3])
    own_w = pltpu.make_async_copy(w.at[x], Wb.at[0], loc.at[0])
    own_a = pltpu.make_async_copy(pairs.at[:, x, z, d], S2.at[pl.ds(2 * j, 2)], loc.at[1])

    def weights():
        for k in sorted(range(1, nx), key=lambda k: -min(k, nx - k)):
            send(w.at[lax.rem(x - k + nx, nx), d], Wb.at[k, d], wx_s.at[k], wx_r.at[k], at_x(x - k))
        yield
        for k in range(1, nx):
            arrived(Wb.at[k, d], wx_s.at[k], wx_r.at[k], at_x(x - k))
        steps = gather_w.steps(w_share)
        next(steps)
        for h in range(2):
            w_share(0, h)
        yield
        yield from steps
        own_w.wait()
        for off in range(ny):
            for h in range(2):
                arrived(w_piece(off, 1 - c, h), wc_s.at[off, h], wc_r.at[off, h], sibling)
        yield

    grads = gather_g.steps(g_share)

    def lora():
        fan_a.start()
        yield
        own_a.wait()
        fan_a.wait()
        for m in range(1, nd):
            other = lax.rem(d + m, nd)
            for s in range(segs):
                sel[m, s] = S2[owner[seg[s, other]]]
            fan_r.send(m)
        for s in range(segs):
            R[s, d] = S2[owner[seg[s, d]]]
        yield
        fan_r.wait()
        tok2 = T[0].reshape(rows, feat)
        cot2 = C[0].reshape(rows, feat)
        part = jnp.zeros((rows, lanes), F32)
        for s in range(segs):
            pair = R[s].reshape(feat, lanes)
            both = jnp.where(lane < rank, dot(tok2, pair), dot(cot2, pair))
            part = part + jnp.where(mask(s), both, 0.0)
        Lp[...] = part.reshape(Lp.shape)
        fan_lx.start()
        yield
        fan_lx.wait()
        total = Lp[x]
        for k in range(1, nx):
            total = total + X1[k]
        Lz[...] = total.reshape(Lz.shape).astype(BF16)
        fan_lz.start()
        yield
        fan_lz.wait()
        total = Lz[z].astype(F32)
        for m in range(1, nz):
            total = total + Z1[m].astype(F32)
        Lf[x, z] = pltpu.roll(total, rank, 1).astype(BF16)
        fan_fz.start()
        yield
        fan_fz.wait()
        fan_fx.start()
        yield
        fan_fx.wait()
        both = Lf[...].reshape(rows, lanes)
        for s in range(segs):
            Lm[:, s * lanes:(s + 1) * lanes] = jnp.where(mask(s), both, jnp.zeros_like(both))
        g_tok = dot(T[0].reshape(rows, feat), Lm[...], TN)
        g_cot = dot(C[0].reshape(rows, feat), Lm[...], TN)
        g_lane = lax.broadcasted_iota(jnp.int32, (feat, lanes), 1)
        for s in range(segs):
            part_s = slice(s * lanes, (s + 1) * lanes)
            G[0, s] = jnp.where(g_lane < rank, g_tok[:, part_s], g_cot[:, part_s]).astype(BF16)
        next(grads)
        for h in range(2):
            g_share(0, h)
        yield

    def fix():
        fix_out = jnp.zeros((rows, feat), F32)
        fix_ig = jnp.zeros((rows, feat), F32)
        for s in range(segs):
            pair = R[s].reshape(feat, lanes)
            mine = Lm[:, s * lanes:(s + 1) * lanes]
            zero = jnp.zeros_like(mine)
            fix_out = fix_out + dot(jnp.where(lane < rank, zero, mine), pair, NT)
            fix_ig = fix_ig + dot(jnp.where(lane < rank, mine, zero), pair, NT)
        acc[0] = acc[0] + fix_out.reshape(2, half_rows, feat)
        Pz[0] = Pz[0] + fix_ig.reshape(2, half_rows, feat)
        yield

    slots = grad.shape[0]
    chunk = min(32, feat)

    def add_grads(i, first):
        off, core = i // CORES, i % CORES
        src = lax.rem(y + off, ny) * CORES + jnp.where(core == 0, c, 1 - c)
        hit = [[(owner[seg[s, src]] == slots * d + q).astype(F32) for s in range(segs)]
               for q in range(slots)]

        def body(r, carry):
            at = pl.ds(pl.multiple_of(r * chunk, chunk), chunk)
            given = [G[i, s, at].astype(F32) for s in range(segs)]
            for q in range(slots):
                value = given[0] * hit[q][0]
                for s in range(1, segs):
                    value = value + given[s] * hit[q][s]
                grad[q, at] = value if first else grad[q, at] + value
            return carry

        lax.fori_loop(0, feat // chunk, body, 0)

    def slots_grad():
        def add(first, count, stride):
            def body(i, carry):
                add_grads(first + i * stride, False)
                return carry

            lax.fori_loop(0, count, body, 0)

        def shared(off):
            for h in range(2):
                arrived(g_piece(off, 1, h), gc_s.at[off, h], gc_r.at[off, h], sibling)

        add_grads(0, True)
        shared(0)
        add(1, 1, 1)
        yield
        if ny > 2:
            add(CORES, 2, CORES * (ny - 2))
            yield
        add(ny, 1, 1)
        for off in range(1, ny):
            if 2 * off != ny:
                shared(off)
        add(CORES + 1, 2 if ny > 2 else 0, CORES * (ny - 2))
        shared(ny // 2)
        add(ny + 1, 1, 1)
        yield

    def partial_ig(off):
        tile = lax.rem(z + off, nz)
        total = jnp.zeros((rows, feat), F32)
        for k in range(nx):
            total = total + dot(C[k].reshape(rows, feat), Wb[k, tile].reshape(feat, feat), NT)
        Pz[off] = total.reshape(2, half_rows, feat)

    def igs():
        def ways(m):
            def body(i, carry):
                partial_ig(m + i * (nz - 2 * m))
                return carry

            lax.fori_loop(0, 2, body, 0)

        partial_ig(nz // 2)
        yield
        for m in range(nz // 2 - 1, 0, -1):
            ways(m)
            yield
        partial_ig(0)
        yield

    def partial_out(m, first):
        tile = lax.rem(z + m, nz)
        block = T[m].reshape(rows, feat)

        def body(k, carry):
            value = dot(block, Wb[k, tile].reshape(feat, feat)).reshape(2, half_rows, feat)
            acc[k] = value if first else acc[k] + value
            return carry

        lax.fori_loop(0, nx, body, 0)

    def outs():
        def ways(m):
            def body(i, carry):
                partial_out(m + i * (nz - 2 * m), False)
                return carry

            lax.fori_loop(0, 2, body, 0)

        partial_out(0, True)
        yield
        for m in range(1, nz // 2):
            ways(m)
            yield
        partial_out(nz // 2, False)
        yield

    for copy in own_s:
        copy.start()
    own_t.start()
    own_c.start()
    own_a.start()
    own_w.start()

    barrier = pltpu.get_barrier_semaphore()
    partners = (
        [at_mp(m) for m in range(1, nx * nz)]
        + [at_dp(d + m) for m in range(1, nd)]
    )
    for device in partners:
        pl.semaphore_signal(barrier, inc=1, device_id=device, device_id_type=pl.DeviceIdType.MESH)
    pl.semaphore_wait(barrier, len(partners))
    for copy in own_s:
        copy.wait()
    own_t.wait()
    own_c.wait()
    for s in range(segs):
        starts.append(starts[-1] + lens[0, s])

    tasks = {
        "W": weights(), "T": gather_t.steps(), "C": gather_c.steps(), "L": lora(), "F": fix(), "G": grads,
        "S": slots_grad(), "i": igs(), "I": scatter_z.steps(ig), "o": outs(), "O": scatter_x.steps(out),
    }
    for name in SCHEDULE:
        next(tasks[name], None)
    for task in tasks.values():
        for _ in task:
            pass

    for copy in pending:
        copy.wait_send()


def local(tokens, base_weight, adapter_pairs, owner_map, seg_adapter, seg_lengths, cotangent):
    rows, feat = tokens.shape
    half = rows // 2
    nz = NZ
    nx = lax.axis_size("mp") // nz
    ny = lax.axis_size("dp") // CORES
    nd = ny * CORES
    stored, depth, lanes = adapter_pairs.shape
    segs = seg_lengths.shape[1]
    total_slots = stored * nx * nz
    slots = total_slots // nd
    piece = feat // nd
    lrows = rows // (nx * nz)
    vmem = lambda shape, dtype: pltpu.VMEM(shape, dtype)
    dma = lambda *shape: pltpu.SemaphoreType.DMA(shape)
    ring = lambda n, pieces=1: [dma(2, 2, pieces, n // 2)] * 2
    pair = lambda *shape: [dma(*shape)] * 2
    scratch = [
        pltpu.SMEM(owner_map.shape, jnp.int32),
        pltpu.SMEM((segs, nd), jnp.int32),
        pltpu.SMEM(seg_lengths.shape, jnp.int32),
        vmem((nz, 2, half, feat), BF16),
        vmem((nx, 2, half, feat), BF16),
        vmem((nx, nz, 2, feat // 2, feat), BF16),
        vmem((total_slots, piece, lanes), BF16),
        vmem((nd, segs, piece, lanes), BF16),
        vmem((segs, nd, piece, lanes), BF16),
        vmem((nx, rows // nx, lanes), F32),
        vmem((nx, rows // nx, lanes), F32),
        vmem((nz, lrows, lanes), BF16),
        vmem((nz, lrows, lanes), BF16),
        vmem((nx, nz, lrows, lanes), BF16),
        vmem((rows, segs * lanes), BF16),
        vmem((nx, 2, half, feat), F32),
        vmem((nz, 2, half, feat), F32),
        vmem((2, 2, nz // 2, half, feat), BF16),
        vmem((2, 2, nz // 2, half, feat), BF16),
        vmem((2, 2, nx // 2, half, feat), BF16),
        vmem((2, 2, nx // 2, half, feat), BF16),
        vmem((nd, segs, feat, lanes), BF16),
        *ring(nz, QT), *ring(nx), *pair(nx), *ring(ny), *pair(ny, 2),
        *pair(nx * nz), *pair(nd), *pair(nx), *pair(nz), *pair(nz), *pair(nx),
        *ring(nz, QI), *ring(nx), *ring(ny), *pair(ny, 2), dma(7),
    ]
    in_vmem = pl.BlockSpec(memory_space=pltpu.VMEM)
    in_any = pl.BlockSpec(memory_space=pl.ANY)
    both, grad = pl.pallas_call(
        functools.partial(kernel, nx, nz, ny),
        out_shape=[
            pltpu.VMEM((4, half, feat), BF16),
            pltpu.VMEM((slots, feat, lanes), F32),
        ],
        in_specs=[in_any] * 7,
        out_specs=[in_vmem] * 2,
        scratch_shapes=scratch,
        compiler_params=pltpu.CompilerParams(
            collective_id=0, has_side_effects=True, vmem_limit_bytes=56 * 1024 * 1024
        ),
    )(
        tokens.reshape(2, half, feat),
        cotangent.reshape(2, half, feat),
        base_weight.reshape(nx, nz, 2, feat // 2, feat),
        adapter_pairs.reshape(stored, nx, nz, nd, piece, lanes),
        owner_map,
        seg_adapter.T,
        seg_lengths,
    )
    both = both.reshape(2, rows, feat)
    return both[0], both[1], grad


def solution(mesh):
    in_specs = (
        P("dp", "mp"),
        P(None, "mp"),
        P("mp", None, None),
        P(),
        P(),
        P("dp", None),
        P("dp", "mp"),
    )
    out_specs = (P("dp", "mp"), P("dp", "mp"), P("dp", "mp", None))
    return jax.shard_map(local, mesh=mesh, in_specs=in_specs, out_specs=out_specs, check_vma=False)
```
